1024 devices in a mesh: comp: 4 (over y), tile: 32 (over z_lo, core), lev: 8 (over z_hi, x).
Axes of the slice: x: 4, y: 4, z: 32 (z_hi: 2, z_lo: 16; z = z_hi * 16 + z_lo), core: 2. Of those that a mesh axis runs over, the one named last changes fastest.
Arguments:
- thermal_anomaly: float32 [4, 80, 16384], P('comp', 'lev', 'tile'), may hold values from -6 to 6
- right_face_transport_ratio: float32 [4, 80, 16384], P('comp', 'lev', 'tile'), may hold values from -0.45 to 0.45
- species_ratios: float32 [4, 40, 80, 16384], P('comp', None, 'lev', 'tile'), may hold values from 0.1 to 3
- lateral_spreading_number: float32 [4, 80, 16384], P('comp', 'lev', 'tile'), may hold values from 0.05 to 0.2
- depth_physics_operator: float32 [4, 80, 80], P('comp'), may hold values from -1 to 1, as said below
- exchange_weight_table: float32 [16384, 4], P('tile'), may hold values from 0.05 to 0.5
- sky_point_of_entry: int32 [16384, 4], P('tile'), may hold values from 0 to 16383, as said below
- water_indicator: int32 [16384], P('tile'), may hold values 0 or 1
Outputs:
- thermal_anomaly_ending: float32 [4, 80, 16384], P('comp', 'lev', 'tile')
- species_ratios_ending: float32 [4, 40, 80, 16384], P('comp', None, 'lev', 'tile')
The draws below stay inside these ranges and needn't reach their ends.
Inputs may be any that keep to these rules, and one draw needn't show every extreme that they name: The ocean cells of each block of 512 (cells b * 512 to (b + 1) * 512 - 1) take their sources near the matching cells of one atmosphere block p(b), p a permutation of the blocks: sky_point_of_entry[j, k] lies cyclically within 128 cells of p(b) * 512 + (j mod 512). `depth_physics_operator`: each matrix has diagonal entries between 0.5 and 1.
All inputs are finite; a program needn't handle non-finite values. No bound on the sum of `water_indicator` on one device may be relied on, other than what follows from the above.
Results may differ from the reference program's by a relative error of at most 0.0003.
Values sent between devices are 32-bit elements; how exact they have to be, the bound alone decides.
A program may use at most 32 MiB of HBM per device.

```python
import math
import jax
import jax.numpy as jnp
from jax import lax

CELLS = 512
DEPTH_LAYERS = 80
NTRAC = 40
NFLUX = 4
OVER = 4
DOMAIN_PARTS = 4
PART_POINTS = 16384


def draw_depth_physics_operator(key, part):
    key_diag = jax.random.fold_in(key, 11)
    key_off = jax.random.fold_in(key, 12)
    diagonal = jax.random.uniform(key_diag, (DOMAIN_PARTS, DEPTH_LAYERS), jnp.float32, 0.5, 1.0)
    spread = 0.35 / jnp.sqrt(jnp.float32(DEPTH_LAYERS))
    offside = jax.random.normal(key_off, (DOMAIN_PARTS, DEPTH_LAYERS, DEPTH_LAYERS), jnp.float32) * spread
    offside = jnp.clip(offside, -0.45, 0.45)
    identity = jnp.eye(DEPTH_LAYERS, dtype=jnp.float32)
    return offside * (1.0 - identity) + diagonal[:, :, None] * identity


def draw_sky_point_of_entry(key, part):
    key_perm = jax.random.fold_in(key, 21)
    key_sign = jax.random.fold_in(key, 22)
    key_free = jax.random.fold_in(key, 23)
    blocks = PART_POINTS // CELLS
    reach = CELLS // 4
    block_map = jax.random.permutation(key_perm, blocks).astype(jnp.int32)
    cell_index = jnp.arange(PART_POINTS, dtype=jnp.int32)
    centre = block_map[cell_index // CELLS] * CELLS + cell_index % CELLS
    sign = jax.random.randint(key_sign, (PART_POINTS,), 0, 2).astype(jnp.int32) * 2 - 1
    free_offset = jax.random.randint(key_free, (PART_POINTS,), -reach, reach + 1).astype(jnp.int32)
    offsets = jnp.stack([jnp.zeros((PART_POINTS,), jnp.int32), sign * reach, -sign * reach, free_offset], 1)
    return ((centre[:, None] + offsets) % PART_POINTS).astype(jnp.int32)


def place_ends(values, key, smallest, largest):
    dims = values.shape
    index_at = [jax.random.randint(jax.random.fold_in(key, axis), (), 0, dims[axis]) for axis in range(len(dims))]
    values = values.at[tuple(index_at)].set(smallest)
    longest = dims.index(max(dims))
    index_at[longest] = (index_at[longest] + 1) % dims[longest]
    return values.at[tuple(index_at)].set(largest)


def block_levels(rng, shape, cuts, smallest, high):
    def one(axis_at, parts):
        steps = jax.random.uniform(jax.random.fold_in(jax.random.fold_in(rng, 6), axis_at), (parts,), jnp.float32, smallest / len(cuts), high / len(cuts))
        return jnp.repeat(jnp.exp(steps), shape[axis_at] // parts).reshape((-1,) + (1,) * (len(shape) - axis_at - 1))

    level = one(*cuts[0])
    for cut in cuts[1:]:
        level = level * one(*cut)
    return level


def gaussian(own_key, shape, deviation, limit, split=(), kind=jnp.bfloat16):
    loudness = block_levels(own_key, shape, split, -0.22, 0.18) if split else 1.0
    drawn = jax.random.normal(own_key, shape, jnp.float32) * deviation * loudness
    return jnp.minimum(jnp.maximum(drawn, -limit), limit).astype(kind)


def setup_inputs(seed: int = 0) -> dict:
    arg_keys = jax.random.split(jax.random.key(seed), 9)
    return {
        "thermal_anomaly": gaussian(arg_keys[0], (DOMAIN_PARTS, DEPTH_LAYERS, PART_POINTS), 1.0, 6.0, ((0, 4), (1, 8), (2, 32)), jnp.float32),
        "right_face_transport_ratio": jnp.clip(jax.random.uniform(arg_keys[1], (DOMAIN_PARTS, DEPTH_LAYERS, PART_POINTS), jnp.float32, -0.45, 0.45) * block_levels(arg_keys[1], (DOMAIN_PARTS, DEPTH_LAYERS, PART_POINTS), ((0, 4), (1, 8), (2, 32)), -0.4, 0.0), -0.45, 0.45),
        "species_ratios": jnp.clip(jnp.exp(math.log(3.0) - 3.4011974 * jax.random.uniform(arg_keys[2], (DOMAIN_PARTS, NTRAC, DEPTH_LAYERS, PART_POINTS), jnp.float32) ** block_levels(arg_keys[2], (DOMAIN_PARTS, NTRAC, DEPTH_LAYERS, PART_POINTS), ((0, 4), (2, 8), (3, 32)), -0.2, 0.2)), 0.1, 3.0),
        "lateral_spreading_number": jnp.clip(0.05 + 0.15 * jax.random.uniform(arg_keys[3], (DOMAIN_PARTS, DEPTH_LAYERS, PART_POINTS), jnp.float32) ** block_levels(arg_keys[3], (DOMAIN_PARTS, DEPTH_LAYERS, PART_POINTS), ((0, 4), (1, 8), (2, 32)), -0.2, 0.2), 0.05, 0.2),
        "depth_physics_operator": draw_depth_physics_operator(jax.random.fold_in(arg_keys[8], 71), 0),
        "exchange_weight_table": jnp.clip(jnp.exp(math.log(0.5) - 2.3025851 * jax.random.uniform(arg_keys[5], (PART_POINTS, OVER), jnp.float32) ** block_levels(arg_keys[5], (PART_POINTS, OVER), ((0, 32),), -0.2, 0.2)), 0.05, 0.5),
        "sky_point_of_entry": draw_sky_point_of_entry(jax.random.fold_in(arg_keys[8], 71), 0),
        "water_indicator": place_ends((jax.random.randint(arg_keys[7], (PART_POINTS,), 0, 4) < 3).astype(jnp.int32), jax.random.fold_in(arg_keys[7], 1), 0, 1),
    }


def advect(field, speed):
    speed_left = jnp.roll(speed, 1, -1)
    flux_right = jnp.maximum(speed, 0.0) * field + jnp.minimum(speed, 0.0) * jnp.roll(field, -1, -1)
    flux_left = jnp.maximum(speed_left, 0.0) * jnp.roll(field, 1, -1) + jnp.minimum(speed_left, 0.0) * field
    return -(flux_right - flux_left)


def one_step(thermal_energy, speed, tracer_set, lateral_spreading_number):
    heat_next = thermal_energy + (advect(thermal_energy, speed) + lateral_spreading_number * (jnp.roll(thermal_energy, 1, -1) - 2.0 * thermal_energy + jnp.roll(thermal_energy, -1, -1)))
    tracer_next = tracer_set + advect(tracer_set, speed[None])
    return heat_next, tracer_next


def domain_part_advance(items):
    thermal_energy, speed, tracer_set, lateral_spreading_number, sky_indicator = items
    thermal_energy, tracer_set = one_step(thermal_energy, speed, tracer_set, lateral_spreading_number)
    heat_two, tracer_two = one_step(thermal_energy, speed, tracer_set, lateral_spreading_number)
    thermal_energy = jnp.where(sky_indicator, heat_two, thermal_energy)
    tracer_set = jnp.where(sky_indicator, tracer_two, tracer_set)
    return thermal_energy, tracer_set


def reference(thermal_anomaly, right_face_transport_ratio, species_ratios, lateral_spreading_number, depth_physics_operator, exchange_weight_table, sky_point_of_entry, water_indicator):
    sky_indicator = jnp.arange(DOMAIN_PARTS) < DOMAIN_PARTS // 2
    thermal_energy, species_group = lax.map(domain_part_advance, (thermal_anomaly, right_face_transport_ratio, species_ratios, lateral_spreading_number, sky_indicator))
    blended_profiles = jnp.einsum("sij,sjn->sin", depth_physics_operator, thermal_energy, precision=lax.Precision.HIGHEST)
    surface = jnp.concatenate([blended_profiles[:, 0:1], species_group[:, 0:NFLUX - 1, 0]], 1)
    received = jnp.roll(surface, DOMAIN_PARTS // 2, axis=0)
    picked = received[:, :, sky_point_of_entry]
    remapped = jnp.sum(picked * exchange_weight_table, -1)
    updated = surface + 0.5 * (remapped - surface)
    is_sea = jnp.logical_and(jnp.logical_not(sky_indicator)[:, None, None], (water_indicator == 1)[None, None, :])
    renewed_interface_values = jnp.where(is_sea, updated, surface)
    thermal_anomaly_ending = blended_profiles.at[:, 0].set(renewed_interface_values[:, 0])
    species_ratios_ending = species_group.at[:, 0:NFLUX - 1, 0].set(renewed_interface_values[:, 1:])
    return thermal_anomaly_ending, species_ratios_ending
```

```python
import functools

import jax
import jax.numpy as jnp
from jax import lax
from jax.experimental import pallas as pl
from jax.experimental.pallas import tpu as pltpu
from jax.sharding import PartitionSpec as P

MESH = pl.DeviceIdType.MESH
F32 = jnp.float32
HIGHEST = lax.Precision.HIGHEST


def dot(a, b):
    return jnp.dot(a, b, precision=HIGHEST, preferred_element_type=F32)


def flux(q, up, un):
    n = q.shape[1]
    return up * q + un * pltpu.roll(q, n - 1, 1)


def tracer_step(q, up, un):
    f = flux(q, up, un)
    return q - (f - pltpu.roll(f, 1, 1))


def heat_step(t, up, un, d):
    n = t.shape[1]
    f = flux(t, up, un)
    return t + (
        -(f - pltpu.roll(f, 1, 1)) + d * (pltpu.roll(t, 1, 1) - 2.0 * t + pltpu.roll(t, n - 1, 1))
    )


def kernel(
    t_hbm, u_hbm, d_hbm, q_hbm, m_ref, w_hbm, i_hbm, sea_hbm,
    tout_hbm, qout_hbm,
    t40, u40, d40, qin, qout, w_v, i_v, i_s, sea_v,
    ext, coef, sendA, sendB, haloA, haloB, gath, flip_s, flip_r, own, srow, piece, rows, pieces, out40,
    in_sem, q_sem, sA, rA, sB, rB, sX, rX, sF, rF, sR, rR, sP, rP, o_sem,
):
    comp, tile, lev = lax.axis_index("comp"), lax.axis_index("tile"), lax.axis_index("lev")
    tiles = lax.axis_size("tile")
    half, x = lev // 4, lax.rem(lev, 4)
    is_sky = comp < 2
    is_target = jnp.logical_and(comp >= 2, lev == 0)
    left, right = lax.rem(tile + tiles - 1, tiles), lax.rem(tile + 1, tiles)
    x_peers = [half * 4 + lax.rem(x + k, 4) for k in range(1, 4)]
    other = lax.rem(lev + 4, 8)

    loads = [
        pltpu.make_async_copy(t_hbm, t40, in_sem.at[0]),
        pltpu.make_async_copy(u_hbm, u40, in_sem.at[1]),
        pltpu.make_async_copy(d_hbm, d40, in_sem.at[2]),
        pltpu.make_async_copy(q_hbm, qin, q_sem),
        pltpu.make_async_copy(w_hbm, w_v, in_sem.at[3]),
        pltpu.make_async_copy(i_hbm, i_v, in_sem.at[4]),
        pltpu.make_async_copy(i_hbm, i_s, in_sem.at[5]),
        pltpu.make_async_copy(sea_hbm, sea_v, in_sem.at[6]),
    ]
    for c in loads:
        c.start()

    bar = pltpu.get_barrier_semaphore()

    def hello(**where):
        pl.semaphore_signal(bar, inc=1, device_id=where, device_id_type=MESH)

    hello(tile=left)
    hello(tile=right)
    for p in x_peers:
        hello(lev=p)
    hello(lev=other)

    @pl.when(is_target)
    def _():
        def body(k, _):
            for j in range(8):
                hello(comp=comp - 2, tile=lax.rem(tile + k, tiles), lev=j)
            return 0

        lax.fori_loop(0, tiles, body, 0)

    def iota(shape, dim):
        return lax.broadcasted_iota(jnp.int32, shape, dim)

    i, j = iota((48, 80), 0), iota((48, 80), 1)
    wanted = jnp.where(i < 16, lev * 10 + i, jnp.where(i < 32, other * 10 + i - 16, i - 32))
    used = jnp.where(i < 16, i, jnp.where(i < 32, i - 16, i - 23)) < 10
    pick_rows = jnp.where(jnp.logical_and(used, wanted == j), 1.0, 0.0).astype(F32)
    i, j = iota((80, 64), 0), iota((80, 64), 1)
    r = lax.rem(j, 16)
    pick_cols = jnp.where(
        jnp.logical_and(r < 10, i == half * 40 + (j // 16) * 10 + r), 1.0, 0.0
    ).astype(F32)
    matrix = dot(dot(pick_rows, m_ref[...]), pick_cols)

    lane = iota((16, 128), 1)
    row = iota((16, 128), 0)

    for c in loads[:3]:
        c.wait()
    blank = jnp.zeros((16, 640), F32)
    for k in range(3):
        ext[k] = blank
    for k, ref in enumerate((t40, u40, d40)):
        for c in range(4):
            ext[k, 0:10, c * 128 : (c + 1) * 128] = ref[pl.ds(c, 10, stride=4), :]
    ends = [ext[k, :, 384:512] for k in range(3)]
    starts = [ext[k, :, 0:128] for k in range(3)]
    sendA[0] = jnp.where(
        lane >= 124, ends[0], jnp.where(lane >= 120, pltpu.roll(ends[1], 124, 1), pltpu.roll(ends[2], 120, 1))
    )
    sendA[1] = jnp.where(
        lane < 4, starts[0], jnp.where(lane < 8, pltpu.roll(starts[1], 4, 1), pltpu.roll(starts[2], 8, 1))
    )
    loads[3].wait()
    lane40 = iota((40, 128), 1)

    def pack(r, carry):
        to_right, to_left = carry
        mine = jnp.logical_and(lane40 >= 2 * r, lane40 < 2 * r + 2)
        to_right = jnp.where(mine, pltpu.roll(qin[r, :, 384:512], 2 * r + 2, 1), to_right)
        to_left = jnp.where(mine, pltpu.roll(qin[r, :, 0:128], 2 * r, 1), to_left)
        return to_right, to_left

    zero40 = jnp.zeros((40, 128), F32)
    to_right, to_left = lax.fori_loop(0, 10, pack, (zero40, zero40))
    sendB[0] = to_right
    sendB[1] = to_left

    pl.semaphore_wait(bar, 6 + jnp.where(is_sky, tiles, 0))

    def send(src, dst, s, r, **where):
        c = pltpu.make_async_remote_copy(
            src_ref=src, dst_ref=dst, send_sem=s, recv_sem=r, device_id=where, device_id_type=MESH
        )
        c.start()
        return c

    edges = [
        send(sendA.at[0], haloA.at[0], sA.at[0], rA.at[0], tile=right),
        send(sendA.at[1], haloA.at[1], sA.at[1], rA.at[1], tile=left),
        send(sendB.at[0], haloB.at[0], sB.at[0], rB.at[0], tile=right),
        send(sendB.at[1], haloB.at[1], sB.at[1], rB.at[1], tile=left),
    ]
    for c in edges:
        c.wait()
    from_left, from_right = haloA[0], haloA[1]
    low = lane < 64
    ext[0, :, 512:640] = jnp.where(low, from_right, from_left)
    ext[1, :, 512:640] = jnp.where(low, pltpu.roll(from_right, 124, 1), pltpu.roll(from_left, 4, 1))
    ext[2, :, 512:640] = jnp.where(low, pltpu.roll(from_right, 120, 1), pltpu.roll(from_left, 8, 1))
    sky = jnp.where(is_sky, 1.0, 0.0).astype(F32)
    up, un = jnp.maximum(ext[1], 0.0), jnp.minimum(ext[1], 0.0)
    coef[0] = up
    coef[1] = un
    coef[2] = up * sky
    coef[3] = un * sky
    heat = heat_step(ext[0], up, un, ext[2])
    heat = heat_step(heat, up * sky, un * sky, ext[2] * sky)[:, 0:512]

    low40 = lane40 < 64

    def level(r):
        edge = jnp.where(
            low40,
            pltpu.roll(haloB[1], lax.rem(128 - 2 * r, 128), 1),
            pltpu.roll(haloB[0], 126 - 2 * r, 1),
        )
        q = jnp.concatenate([qin[r], edge], axis=1)
        up, un, up2, un2 = (jnp.broadcast_to(coef[k, pl.ds(r, 1), :], (40, 640)) for k in range(4))
        q = tracer_step(tracer_step(q, up, un), up2, un2)
        qout[r] = q[:, 0:512]

    level(0)
    row8 = iota((8, 512), 0)
    rows_q = pltpu.roll(qout[0, 0:8, :], 2, 0)
    gath[x, 0:8, :] = heat[0:8]
    gath[x, 8:16, :] = jnp.where(row8 < 2, heat[8:16], jnp.where(row8 < 5, rows_q, 0.0))
    shares = [send(gath.at[x], gath.at[x], sX.at[k], rX.at[k], lev=x_peers[k]) for k in range(3)]
    for c in shares:
        c.wait()
    product = dot(matrix, jnp.concatenate([gath[k] for k in range(4)], axis=0))
    own[...] = product[0:16]
    for c in range(4):
        flip_s[pl.ds(c, 10, stride=4), :] = product[16:26, c * 128 : (c + 1) * 128]
    top = product[32:33, :]
    line = jnp.where(
        x == 0, gath[0, 10:11, :], jnp.where(x == 1, gath[0, 11:12, :], jnp.where(x == 2, gath[0, 12:13, :], top))
    )
    for c in range(4):
        srow[c : c + 1, :] = line[:, c * 128 : (c + 1) * 128]
    piece[...] = jnp.where(
        x == 0, top[:, 0:128], jnp.where(x == 1, top[:, 128:256], jnp.where(x == 2, top[:, 256:384], top[:, 384:512]))
    )

    flip = send(flip_s, flip_r, sF, rF, lev=other)

    @pl.when(jnp.logical_and(is_sky, half == 0))
    def _():
        def body(k, _):
            send(srow, rows.at[x, tile], sR, rR, comp=comp + 2, tile=lax.rem(tile + k, tiles), lev=0)
            return 0

        lax.fori_loop(0, tiles, body, 0)

    @pl.when(jnp.logical_and(is_sky, half == 1))
    def _():
        def body(k, _):
            send(piece, pieces.at[x, tile], sP, rP, comp=comp + 2, tile=lax.rem(tile + k, tiles), lev=0)
            return 0

        lax.fori_loop(0, tiles, body, 0)

    def more(r, _):
        level(r)
        pltpu.make_async_copy(qout.at[r], qout_hbm.at[r], o_sem.at[0]).start()
        return 0

    lax.fori_loop(1, 10, more, 0)

    flip.wait()
    for c in range(4):
        out40[pl.ds(c, 10, stride=4), :] = own[0:10, c * 128 : (c + 1) * 128] + flip_r[pl.ds(c, 10, stride=4), :]

    for c in loads[4:]:
        c.wait()

    @pl.when(is_target)
    def _():
        pltpu.make_async_copy(rows, rows, rR).wait()
        pltpu.make_async_copy(pieces, pieces, rP).wait()
        block = lax.shift_right_logical(i_s[0, 256], 9)
        before, after = lax.rem(block + tiles - 1, tiles), lax.rem(block + 1, tiles)
        window = []
        for f in range(4):
            b, m, a = rows[f, before], rows[f, block], rows[f, after]
            window.append([b[3:4]] + [m[c : c + 1] for c in range(4)] + [a[0:1]])
        extra = [pieces[3, before]] + [pieces[c, block] for c in range(4)] + [pieces[0, after]]
        window[3] = [a + b for a, b in zip(window[3], extra)]
        for c in range(4):
            at = slice(c * 128, (c + 1) * 128)
            place = jnp.bitwise_and(i_v[:, at] - block * 512 + 128, tiles * 512 - 1)
            place = jnp.concatenate([place, place], axis=0)
            which, within = lax.shift_right_logical(place, 7), jnp.bitwise_and(place, 127)
            weight = w_v[:, at]
            sea = sea_v[c : c + 1, :] == 1
            for pair in ((0, 1), (2, 3)):
                got = jnp.zeros((8, 128), F32)
                for m in range(c, c + 3):
                    source = jnp.concatenate(
                        [jnp.broadcast_to(window[f][m], (4, 128)) for f in pair], axis=0
                    )
                    taken = jnp.take_along_axis(source, within, axis=1, mode="promise_in_bounds")
                    got = jnp.where(which == m, taken, got)
                for k, f in enumerate(pair):
                    remapped = jnp.sum(got[4 * k : 4 * k + 4] * weight, axis=0, keepdims=True)
                    if f < 3:
                        s = qout[0, f : f + 1, at]
                        qout[0, f : f + 1, at] = jnp.where(sea, s + 0.5 * (remapped - s), s)
                    else:
                        s = out40[c : c + 1, :]
                        out40[c : c + 1, :] = jnp.where(sea, s + 0.5 * (remapped - s), s)

    last = [
        pltpu.make_async_copy(out40, tout_hbm, o_sem.at[1]),
        pltpu.make_async_copy(qout.at[0], qout_hbm.at[0], o_sem.at[2]),
    ]
    for c in last:
        c.start()

    @pl.when(jnp.logical_and(is_sky, half == 0))
    def _():
        pltpu.make_async_copy(rows.at[0], rows.at[0], sR).wait()

    @pl.when(jnp.logical_and(is_sky, half == 1))
    def _():
        pltpu.make_async_copy(pieces.at[0], pieces.at[0], sP).wait()

    pltpu.make_async_copy(qout.at[pl.ds(1, 9)], qout_hbm.at[pl.ds(1, 9)], o_sem.at[0]).wait()
    for c in last:
        c.wait()


def body(t, u, q, d, m, w, i, sea):
    any_ = pl.BlockSpec(memory_space=pl.ANY)
    vmem = pl.BlockSpec(memory_space=pltpu.VMEM)
    dma = pltpu.SemaphoreType.DMA
    tiles = lax.axis_size("tile")
    buf = lambda *s: pltpu.VMEM(s, F32)
    tout, qout = pl.pallas_call(
        kernel,
        out_shape=(jax.ShapeDtypeStruct((40, 128), F32), jax.ShapeDtypeStruct((10, 40, 512), F32)),
        in_specs=[any_, any_, any_, any_, vmem, any_, any_, any_],
        out_specs=(any_, any_),
        scratch_shapes=[
            buf(40, 128), buf(40, 128), buf(40, 128), buf(10, 40, 512), buf(10, 40, 512),
            buf(4, 512), pltpu.VMEM((4, 512), jnp.int32), pltpu.SMEM((4, 512), jnp.int32), pltpu.VMEM((4, 128), jnp.int32),
            buf(3, 16, 640), buf(4, 16, 640), buf(2, 16, 128), buf(2, 40, 128), buf(2, 16, 128), buf(2, 40, 128),
            buf(4, 16, 512), buf(40, 128), buf(40, 128), buf(16, 512), buf(4, 128), buf(1, 128),
            buf(4, tiles, 4, 128), buf(4, tiles, 1, 128), buf(40, 128),
            dma((7,)), dma, dma((2,)), dma((2,)), dma((2,)), dma((2,)), dma((3,)), dma((3,)), dma, dma,
            dma, dma, dma, dma, dma((3,)),
        ],
        compiler_params=pltpu.CompilerParams(
            collective_id=0, has_side_effects=True, vmem_limit_bytes=24 * 1024 * 1024
        ),
    )(
        t.reshape(40, 128), u.reshape(40, 128), d.reshape(40, 128), jnp.transpose(q[0], (1, 0, 2)),
        m[0], w.T, i.T, sea.reshape(4, 128),
    )
    return tout.reshape(1, 10, 512), jnp.transpose(qout, (1, 0, 2))[None]


def solution(mesh):
    in_specs = (
        P("comp", "lev", "tile"),
        P("comp", "lev", "tile"),
        P("comp", None, "lev", "tile"),
        P("comp", "lev", "tile"),
        P("comp", None, None),
        P("tile", None),
        P("tile", None),
        P("tile"),
    )
    out_specs = (P("comp", "lev", "tile"), P("comp", None, "lev", "tile"))
    return jax.shard_map(body, mesh=mesh, in_specs=in_specs, out_specs=out_specs, check_vma=False)
```

```python
import functools

import jax
import jax.numpy as jnp
from jax import lax
from jax.experimental import pallas as pl
from jax.experimental.pallas import tpu as pltpu
from jax.sharding import PartitionSpec as P

MESH = pl.DeviceIdType.MESH
F32 = jnp.float32
HIGHEST = lax.Precision.HIGHEST


def dot(a, b):
    return jnp.dot(a, b, precision=HIGHEST, preferred_element_type=F32)


def flux(q, up, un):
    n = q.shape[1]
    return up * q + un * pltpu.roll(q, n - 1, 1)


def tracer_step(q, up, un):
    f = flux(q, up, un)
    return q - (f - pltpu.roll(f, 1, 1))


def heat_step(t, up, un, d):
    n = t.shape[1]
    f = flux(t, up, un)
    return t + (
        -(f - pltpu.roll(f, 1, 1)) + d * (pltpu.roll(t, 1, 1) - 2.0 * t + pltpu.roll(t, n - 1, 1))
    )


def drain(ref, sem):
    pltpu.make_async_copy(ref, ref, sem).wait()


def send(src, dst, s, r, **where):
    pltpu.make_async_remote_copy(
        src_ref=src, dst_ref=dst, send_sem=s, recv_sem=r, device_id=where, device_id_type=MESH
    ).start()


def iota(shape, dim):
    return lax.broadcasted_iota(jnp.int32, shape, dim)


def joined(from_right, from_left):
    low = iota((16, 128), 1) < 64
    return (
        jnp.where(low, from_right, from_left),
        jnp.where(low, pltpu.roll(from_right, 124, 1), pltpu.roll(from_left, 4, 1)),
        jnp.where(low, pltpu.roll(from_right, 120, 1), pltpu.roll(from_left, 8, 1)),
    )


def courant(u):
    return jnp.maximum(u, 0.0), jnp.minimum(u, 0.0)


def kernel(
    t_hbm, u_hbm, d_hbm, q_hbm, m_hbm, w_hbm, i_hbm, sea_hbm,
    tout, qout,
    t40, u40, d40, qin, m_v, w_v, i_v, i_s, sea_v,
    ext, coef, sendA, sendB, haloA, haloB, gath, flip_s, flip_r, own, srow, piece, rows, pieces,
    ring, ring_coef, wrapB, edge_s, edge_r, edge_rows,
    in_sem, sA, rA, sB, rB, sX, rX, sF, rF, sR, rR, sP, rP, sE, rE, sW, rW, sG, rG, ready,
):
    comp, tile, lev = lax.axis_index("comp"), lax.axis_index("tile"), lax.axis_index("lev")
    tiles = lax.axis_size("tile")
    half, x = lev // 4, lax.rem(lev, 4)
    is_sky = comp < 2
    is_target = jnp.logical_and(comp >= 2, lev == 0)
    first, last = tile == 0, tile == tiles - 1
    is_wrap = jnp.logical_or(first, last)
    order = half * 2 + jnp.where(last, 1, 0)
    x_peers = [half * 4 + lax.rem(x + k, 4) for k in range(1, 4)]
    other = lax.rem(lev + 4, 8)

    def group(g, k):
        return {"tile": (tiles - 1) * (g % 2), "lev": (g // 2) * 4 + k}

    pairs = (
        (t_hbm, t40), (u_hbm, u40), (d_hbm, d40), (q_hbm, qin), (m_hbm, m_v),
        (w_hbm, w_v), (i_hbm, i_v), (i_hbm, i_s), (sea_hbm, sea_v),
    )
    loads = [pltpu.make_async_copy(a, b, in_sem.at[k]) for k, (a, b) in enumerate(pairs)]
    for c in loads:
        c.start()

    bar = pltpu.get_barrier_semaphore()

    def hello(**where):
        pl.semaphore_signal(bar, inc=1, device_id=where, device_id_type=MESH)

    @pl.when(tile > 0)
    def _():
        hello(tile=tile - 1)

    @pl.when(tile < tiles - 1)
    def _():
        hello(tile=tile + 1)

    for p in x_peers:
        hello(lev=p)

    @pl.when(half == 0)
    def _():
        hello(lev=lev + 4)

    @pl.when(is_wrap)
    def _():
        for g in range(1, 4):

            @pl.when(g > order)
            def _():
                for k in range(4):
                    hello(**group(g, k))

    @pl.when(is_target)
    def _():
        def body(k, _):
            for j in range(8):
                hello(comp=comp - 2, tile=lax.rem(tile + k, tiles), lev=j)
            return 0

        lax.fori_loop(0, tiles, body, 0)

    lane = iota((16, 128), 1)

    blank = jnp.zeros((16, 640), F32)
    for k in range(3):
        ext[k] = blank
    for c in loads[:3]:
        c.wait()
    for k, ref in enumerate((t40, u40, d40)):
        for c in range(4):
            ext[k, 0:10, c * 128 : (c + 1) * 128] = ref[pl.ds(c, 10, stride=4), :]
    ends = [ext[k, :, 384:512] for k in range(3)]
    starts = [ext[k, :, 0:128] for k in range(3)]
    sendA[0] = jnp.where(
        lane >= 124, ends[0], jnp.where(lane >= 120, pltpu.roll(ends[1], 124, 1), pltpu.roll(ends[2], 120, 1))
    )
    sendA[1] = jnp.where(
        lane < 4, starts[0], jnp.where(lane < 8, pltpu.roll(starts[1], 4, 1), pltpu.roll(starts[2], 8, 1))
    )
    loads[3].wait()
    lane40 = iota((40, 128), 1)
    low40 = lane40 < 64
    zero40 = jnp.zeros((40, 128), F32)

    def pack(r, carry):
        to_right, to_left = carry
        mine = jnp.logical_and(lane40 >= 2 * r, lane40 < 2 * r + 2)
        to_right = jnp.where(mine, pltpu.roll(qin[r, :, 384:512], 2 * r + 2, 1), to_right)
        to_left = jnp.where(mine, pltpu.roll(qin[r, :, 0:128], 2 * r, 1), to_left)
        return to_right, to_left

    to_right, to_left = lax.fori_loop(0, 10, pack, (zero40, zero40))
    sendB[0] = to_right
    sendB[1] = to_left

    @pl.when(first)
    def _():
        haloA[0] = jnp.zeros((16, 128), F32)
        haloB[0] = zero40

    @pl.when(last)
    def _():
        haloA[1] = jnp.zeros((16, 128), F32)
        haloB[1] = zero40

    greeted = (
        jnp.where(tile > 0, 1, 0) + jnp.where(tile < tiles - 1, 1, 0) + 3 + half
        + jnp.where(is_sky, tiles, 0) + jnp.where(is_wrap, 4 * order, 0)
    )
    pl.semaphore_wait(bar, greeted)

    @pl.when(tile < tiles - 1)
    def _():
        send(sendA.at[0], haloA.at[0], sA.at[0], rA.at[0], tile=tile + 1)
        send(sendB.at[0], haloB.at[0], sB.at[0], rB.at[0], tile=tile + 1)

    @pl.when(tile > 0)
    def _():
        send(sendA.at[1], haloA.at[1], sA.at[1], rA.at[1], tile=tile - 1)
        send(sendB.at[1], haloB.at[1], sB.at[1], rB.at[1], tile=tile - 1)

    @pl.when(half == 1)
    def _():
        pl.semaphore_signal(ready, inc=1, device_id={"lev": lev - 4}, device_id_type=MESH)

    loads[4].wait()
    i, j = iota((48, 80), 0), iota((48, 80), 1)
    wanted = jnp.where(i < 16, lev * 10 + i, jnp.where(i < 32, other * 10 + i - 16, i - 32))
    used = jnp.where(i < 16, i, jnp.where(i < 32, i - 16, i - 23)) < 10
    pick_rows = jnp.where(jnp.logical_and(used, wanted == j), 1.0, 0.0).astype(F32)

    def pick_cols(count, start):
        i, j = iota((80, count), 0), iota((80, count), 1)
        r = lax.rem(j, 16)
        return jnp.where(jnp.logical_and(r < 10, i == start + (j // 16) * 10 + r), 1.0, 0.0).astype(F32)

    @pl.when(is_wrap)
    def _():
        ring[order, x] = jnp.where(last, sendA[0], sendA[1])
        mine = ring.at[order, x]
        for p in x_peers:
            send(mine, mine, sE.at[order], rE.at[order], lev=p)
        for g in range(0, 3):

            @pl.when(g < order)
            def _():
                for k in range(4):
                    send(mine, mine, sE.at[g], rE.at[order], **group(g, k))

        @pl.when(last)
        def _():
            send(sendB.at[0], wrapB, sW, rW, tile=0)

        @pl.when(is_sky)
        def _():
            i, j = iota((16, 80), 0), iota((16, 80), 1)
            here = jnp.logical_and(i < 10, j == lev * 10 + i)
            scale = jnp.sum(jnp.where(here, jnp.broadcast_to(m_v[0:1, :], (16, 80)), 0.0), axis=1, keepdims=True)
            is_t = jnp.where(last, lane - 124, 3 - lane) >= 0
            edge = ring[order, x]
            edge = jnp.where(is_t, edge * scale, edge)
            q3 = jnp.where(last, qin[0, 0:8, 384:512], qin[0, 0:8, 0:128])
            low8 = iota((8, 128), 0) < 2
            edge_s[0:8] = edge[0:8]
            edge_s[8:16] = jnp.where(low8, edge[8:16], pltpu.roll(q3, 2, 0))
            side = jnp.where(last, 1, 0)

            def body(k, _):
                send(edge_s, edge_r.at[side, lev], sG, rG, comp=comp + 2, tile=lax.rem(tile + k, tiles), lev=0)
                return 0

            lax.fori_loop(0, tiles, body, 0)

    matrix = dot(dot(pick_rows, m_v[...]), pick_cols(64, half * 40))

    @pl.when(tile > 0)
    def _():
        drain(haloA.at[0], rA.at[0])
        drain(haloB.at[0], rB.at[0])

    @pl.when(tile < tiles - 1)
    def _():
        drain(haloA.at[1], rA.at[1])
        drain(haloB.at[1], rB.at[1])

    for k, block in enumerate(joined(haloA[1], haloA[0])):
        ext[k, :, 512:640] = block
    sky = jnp.where(is_sky, 1.0, 0.0).astype(F32)
    up, un = courant(ext[1])
    coef[0] = up
    coef[1] = un
    coef[2] = up * sky
    coef[3] = un * sky
    heat = heat_step(ext[0], up, un, ext[2])
    heat = heat_step(heat, up * sky, un * sky, ext[2] * sky)[:, 0:512]

    def level(r):
        edge = jnp.where(
            low40,
            pltpu.roll(haloB[1], lax.rem(128 - 2 * r, 128), 1),
            pltpu.roll(haloB[0], 126 - 2 * r, 1),
        )
        q = jnp.concatenate([qin[r], edge], axis=1)
        up, un, up2, un2 = (jnp.broadcast_to(coef[k, pl.ds(r, 1), :], (40, 640)) for k in range(4))
        q = tracer_step(tracer_step(q, up, un), up2, un2)
        qout[r] = q[:, 0:512]

    level(0)
    row8 = iota((8, 512), 0)
    rows_q = pltpu.roll(qout[0, 0:8, :], 2, 0)
    gath[x, 0:8, :] = heat[0:8]
    gath[x, 8:16, :] = jnp.where(row8 < 2, heat[8:16], jnp.where(row8 < 5, rows_q, 0.0))
    for k in range(3):
        send(gath.at[x], gath.at[x], sX.at[k], rX.at[k], lev=x_peers[k])
    for k in range(3):
        drain(gath.at[k], rX.at[k])
    product = dot(matrix, jnp.concatenate([gath[k] for k in range(4)], axis=0))
    top = product[32:33, :]

    @pl.when(jnp.logical_and(is_sky, half == 1))
    def _():
        piece[...] = jnp.where(
            x == 0, top[:, 0:128], jnp.where(x == 1, top[:, 128:256], jnp.where(x == 2, top[:, 256:384], top[:, 384:512]))
        )

        def body(k, _):
            send(piece, pieces.at[x, tile], sP, rP, comp=comp + 2, tile=k, lev=0)
            return 0

        lax.fori_loop(0, tiles, body, 0)

    @pl.when(jnp.logical_and(is_sky, half == 0))
    def _():
        line = jnp.where(
            x == 0, gath[0, 10:11, :], jnp.where(x == 1, gath[0, 11:12, :], jnp.where(x == 2, gath[0, 12:13, :], top))
        )
        for c in range(4):
            srow[c : c + 1, :] = line[:, c * 128 : (c + 1) * 128]

        def body(k, _):
            send(srow, rows.at[x, tile], sR, rR, comp=comp + 2, tile=lax.rem(tile + k, tiles), lev=0)
            return 0

        lax.fori_loop(0, tiles, body, 0)

    own[...] = product[0:16]
    for c in range(4):
        flip_s[pl.ds(c, 10, stride=4), :] = product[16:26, c * 128 : (c + 1) * 128]

    @pl.when(half == 1)
    def _():
        send(flip_s, flip_r, sF, rF, lev=other)

    def more(r, _):
        level(r)
        return 0

    lax.fori_loop(1, 10, more, 0)

    @pl.when(half == 0)
    def _():
        pl.semaphore_wait(ready, 1)
        send(flip_s, flip_r, sF, rF, lev=other)

    for c in loads[5:]:
        c.wait()

    @pl.when(is_wrap)
    def _():
        mine = ring.at[order, x]
        for g in range(1, 4):

            @pl.when(g > order)
            def _():
                drain(ring.at[g], rE.at[g])
                for k in range(4):
                    send(mine, mine, sE.at[g], rE.at[order], **group(g, k))

        drain(wrapB, rW)

        @pl.when(first)
        def _():
            send(sendB.at[1], wrapB, sW, rW, tile=tiles - 1)

        drain(ring.at[order, pl.ds(0, 3)], rE.at[order])
        for g in range(0, 3):

            @pl.when(g < order)
            def _():
                drain(ring.at[g], rE.at[g])

        up, un = courant(joined(ring[half * 2, x], ring[half * 2 + 1, x])[1])
        ring_coef[0] = up
        ring_coef[1] = un
        ring_coef[2] = up * sky
        ring_coef[3] = un * sky
        for flag, c, turn in ((first, 0, 126), (last, 3, 128)):

            @pl.when(flag)
            def _():
                def fix(r, _):
                    at = slice(c * 128, (c + 1) * 128)
                    far = pltpu.roll(wrapB[...], lax.rem(turn - 2 * r, 128), 1)
                    q = jnp.where(low40, qin[r, :, at], far) if c == 0 else jnp.where(low40, far, qin[r, :, at])
                    up, un, up2, un2 = (
                        jnp.broadcast_to(ring_coef[k, pl.ds(r, 1), :], (40, 128)) for k in range(4)
                    )
                    q = tracer_step(tracer_step(q, up, un), up2, un2)
                    new = lane40 < 2 if c == 0 else lane40 >= 126
                    qout[r, :, at] = jnp.where(new, q, qout[r, :, at])
                    return 0

                lax.fori_loop(0, 10, fix, 0)

    def edge_heat(from_right, from_left, again):
        t, u, d = joined(from_right, from_left)
        up, un = courant(u)
        return heat_step(heat_step(t, up, un, d), up * again, un * again, d * again)

    @pl.when(is_target)
    def _():
        drain(edge_r, rG)
        total = edge_heat(edge_r[0, 0], edge_r[1, 0], 1.0)
        for k in range(1, 8):
            total = total + edge_heat(edge_r[0, k], edge_r[1, k], 1.0)
        total = jnp.where(iota((16, 128), 0) < 10, total, 0.0)
        q, u, _ = joined(edge_r[0, 0], edge_r[1, 0])
        up, un = courant(jnp.broadcast_to(u[0:1], (8, 128)))
        edge_rows[...] = tracer_step(tracer_step(q[8:16], up, un), up, un)
        edge_rows[0:1, :] = jnp.sum(total, axis=0, keepdims=True)

    block = lax.shift_right_logical(i_s[0, 256], 9)
    before, after = lax.rem(block + tiles - 1, tiles), lax.rem(block + 1, tiles)
    lane1 = iota((1, 128), 1)

    def window(f):
        b, m, a = rows[f, before], rows[f, block], rows[f, after]
        w = [b[3:4]] + [m[c : c + 1] for c in range(4)] + [a[0:1]]
        if f == 3:
            extra = [pieces[3, before]] + [pieces[c, block] for c in range(4)] + [pieces[0, after]]
            w = [a + b for a, b in zip(w, extra)]
        edge = edge_rows[0:1, :] if f == 3 else edge_rows[2 + f : 3 + f, :]
        w[0] = jnp.where(lane1 >= jnp.where(before == tiles - 1, 126, 128), edge, w[0])
        w[1] = jnp.where(lane1 < jnp.where(block == 0, 2, 0), edge, w[1])
        w[4] = jnp.where(lane1 >= jnp.where(block == tiles - 1, 126, 128), edge, w[4])
        w[5] = jnp.where(lane1 < jnp.where(after == 0, 2, 0), edge, w[5])
        return w

    def remap(pair):
        windows = [window(f) for f in pair]
        for c in range(4):
            at = slice(c * 128, (c + 1) * 128)
            place = jnp.bitwise_and(i_v[:, at] - block * 512 + 128, tiles * 512 - 1)
            place = jnp.concatenate([place, place], axis=0)
            which, within = lax.shift_right_logical(place, 7), jnp.bitwise_and(place, 127)
            weight = w_v[:, at]
            sea = sea_v[c : c + 1, :] == 1
            got = jnp.zeros((8, 128), F32)
            for m in range(c, c + 3):
                source = jnp.concatenate([jnp.broadcast_to(w[m], (4, 128)) for w in windows], axis=0)
                taken = jnp.take_along_axis(source, within, axis=1, mode="promise_in_bounds")
                got = jnp.where(which == m, taken, got)
            for k, f in enumerate(pair):
                remapped = jnp.sum(got[4 * k : 4 * k + 4] * weight, axis=0, keepdims=True)
                if f < 3:
                    s = qout[0, f : f + 1, at]
                    qout[0, f : f + 1, at] = jnp.where(sea, s + 0.5 * (remapped - s), s)
                else:
                    s = tout[c : c + 1, :]
                    tout[c : c + 1, :] = jnp.where(sea, s + 0.5 * (remapped - s), s)

    @pl.when(is_target)
    def _():
        drain(rows, rR)
        remap((0, 1))

    drain(flip_r, rF)
    for c in range(4):
        tout[pl.ds(c, 10, stride=4), :] = own[0:10, c * 128 : (c + 1) * 128] + flip_r[pl.ds(c, 10, stride=4), :]

    @pl.when(is_wrap)
    def _():
        mixed_rows = dot(dot(pick_rows[0:16], m_v[...]), pick_cols(128, 0))
        stepped = [edge_heat(ring[2 * (k // 4), k % 4], ring[2 * (k // 4) + 1, k % 4], sky) for k in range(8)]
        mixed = dot(mixed_rows, jnp.concatenate(stepped, axis=0))[0:10]
        for flag, c, new in ((first, 0, lane < 2), (last, 3, lane >= 126)):

            @pl.when(flag)
            def _():
                tout[pl.ds(c, 10, stride=4), :] = jnp.where(new[0:10], mixed, tout[pl.ds(c, 10, stride=4), :])

    @pl.when(is_target)
    def _():
        drain(pieces, rP)
        remap((2, 3))

    @pl.when(tile < tiles - 1)
    def _():
        drain(sendA.at[0], sA.at[0])
        drain(sendB.at[0], sB.at[0])

    @pl.when(tile > 0)
    def _():
        drain(sendA.at[1], sA.at[1])
        drain(sendB.at[1], sB.at[1])

    for k in range(3):
        drain(gath.at[k], sX.at[k])
    drain(flip_s, sF)

    @pl.when(jnp.logical_and(is_sky, half == 0))
    def _():
        drain(rows.at[0], sR)

    @pl.when(jnp.logical_and(is_sky, half == 1))
    def _():
        drain(pieces.at[0], sP)

    @pl.when(is_wrap)
    def _():
        for g in range(4):

            @pl.when(g == order)
            def _():
                drain(ring.at[g, pl.ds(0, 3)], sE.at[g])

            @pl.when(g != order)
            def _():
                drain(ring.at[g], sE.at[g])

        drain(wrapB, sW)

        @pl.when(is_sky)
        def _():
            for k in range(2):
                drain(edge_r, sG)


def body(t, u, q, d, m, w, i, sea):
    hbm = pl.BlockSpec(memory_space=pltpu.HBM)
    vmem = pl.BlockSpec(memory_space=pltpu.VMEM)
    dma = pltpu.SemaphoreType.DMA
    tiles = lax.axis_size("tile")
    buf = lambda *s: pltpu.VMEM(s, F32)
    tout, qout = pl.pallas_call(
        kernel,
        out_shape=(jax.ShapeDtypeStruct((40, 128), F32), jax.ShapeDtypeStruct((10, 40, 512), F32)),
        in_specs=[hbm] * 8,
        out_specs=(vmem, vmem),
        scratch_shapes=[
            buf(40, 128), buf(40, 128), buf(40, 128), buf(10, 40, 512), buf(80, 80),
            buf(4, 512), pltpu.VMEM((4, 512), jnp.int32), pltpu.SMEM((4, 512), jnp.int32), pltpu.VMEM((4, 128), jnp.int32),
            buf(3, 16, 640), buf(4, 16, 640), buf(2, 16, 128), buf(2, 40, 128), buf(2, 16, 128), buf(2, 40, 128),
            buf(4, 16, 512), buf(40, 128), buf(40, 128), buf(16, 512), buf(4, 128), buf(1, 128),
            buf(4, tiles, 4, 128), buf(4, tiles, 1, 128),
            buf(4, 4, 16, 128), buf(4, 16, 128), buf(40, 128), buf(16, 128), buf(2, 8, 16, 128), buf(8, 128),
            dma((9,)), dma((2,)), dma((2,)), dma((2,)), dma((2,)), dma((3,)), dma((3,)), dma, dma,
            dma, dma, dma, dma, dma((4,)), dma((4,)), dma, dma, dma, dma, pltpu.SemaphoreType.REGULAR,
        ],
        compiler_params=pltpu.CompilerParams(
            collective_id=0, has_side_effects=True, vmem_limit_bytes=24 * 1024 * 1024
        ),
    )(
        t.reshape(40, 128), u.reshape(40, 128), d.reshape(40, 128), jnp.transpose(q[0], (1, 0, 2)),
        m[0], w.T, i.T, sea.reshape(4, 128),
    )
    return tout.reshape(1, 10, 512), jnp.transpose(qout, (1, 0, 2))[None]


def solution(mesh):
    in_specs = (
        P("comp", "lev", "tile"),
        P("comp", "lev", "tile"),
        P("comp", None, "lev", "tile"),
        P("comp", "lev", "tile"),
        P("comp", None, None),
        P("tile", None),
        P("tile", None),
        P("tile"),
    )
    out_specs = (P("comp", "lev", "tile"), P("comp", None, "lev", "tile"))
    return jax.shard_map(body, mesh=mesh, in_specs=in_specs, out_specs=out_specs, check_vma=False)
```

```python
import functools

import jax
import jax.numpy as jnp
from jax import lax
from jax.experimental import pallas as pl
from jax.experimental.pallas import tpu as pltpu
from jax.sharding import PartitionSpec as P

MESH = pl.DeviceIdType.MESH
F32 = jnp.float32
HIGHEST = lax.Precision.HIGHEST


def dot(a, b):
    return jnp.dot(a, b, precision=HIGHEST, preferred_element_type=F32)


def flux(q, up, un):
    n = q.shape[1]
    return up * q + un * pltpu.roll(q, n - 1, 1)


def tracer_step(q, up, un):
    f = flux(q, up, un)
    return q - (f - pltpu.roll(f, 1, 1))


def heat_step(t, up, un, d):
    n = t.shape[1]
    f = flux(t, up, un)
    return t + (
        -(f - pltpu.roll(f, 1, 1)) + d * (pltpu.roll(t, 1, 1) - 2.0 * t + pltpu.roll(t, n - 1, 1))
    )


def drain(ref, sem):
    pltpu.make_async_copy(ref, ref, sem).wait()


def send(src, dst, s, r, **where):
    pltpu.make_async_remote_copy(
        src_ref=src, dst_ref=dst, send_sem=s, recv_sem=r, device_id=where, device_id_type=MESH
    ).start()


def iota(shape, dim):
    return lax.broadcasted_iota(jnp.int32, shape, dim)


def joined(from_right, from_left):
    low = iota((16, 128), 1) < 64
    return (
        jnp.where(low, from_right, from_left),
        jnp.where(low, pltpu.roll(from_right, 124, 1), pltpu.roll(from_left, 4, 1)),
        jnp.where(low, pltpu.roll(from_right, 120, 1), pltpu.roll(from_left, 8, 1)),
    )


def courant(u):
    return jnp.maximum(u, 0.0), jnp.minimum(u, 0.0)


def kernel(
    t_hbm, u_hbm, d_hbm, q_hbm, m_hbm, w_hbm, i_hbm, sea_hbm,
    tout, qout,
    t40, u40, d40, qin, m_v, w_v, i_v, i_s, sea_v,
    ext, coef, sendA, sendB, haloA, haloB, gath, flip_s, flip_r, own, srow, piece, rows, pieces,
    ring, ring_coef, wrapB, edge_s, edge_rows, mixed_rows, mixed_v,
    in_sem, sA, rA, sB, rB, sX, rX, sF, rF, sR, rR, sP, rP, sE, rE, sW, rW, sG, rG, ready,
):
    comp, tile, lev = lax.axis_index("comp"), lax.axis_index("tile"), lax.axis_index("lev")
    tiles = lax.axis_size("tile")
    half, x = lev // 4, lax.rem(lev, 4)
    is_sky = comp < 2
    is_target = jnp.logical_and(comp >= 2, lev == 0)
    first, last = tile == 0, tile == tiles - 1
    is_wrap = jnp.logical_or(first, last)
    order = half * 2 + jnp.where(last, 1, 0)
    x_peers = [half * 4 + lax.rem(x + k, 4) for k in range(1, 4)]
    other = lax.rem(lev + 4, 8)

    def group(g, k):
        return {"tile": (tiles - 1) * (g % 2), "lev": (g // 2) * 4 + k}

    pairs = (
        (t_hbm, t40), (u_hbm, u40), (d_hbm, d40), (q_hbm, qin), (m_hbm, m_v),
        (w_hbm, w_v), (i_hbm, i_v), (i_hbm, i_s), (sea_hbm, sea_v),
    )
    loads = [pltpu.make_async_copy(a, b, in_sem.at[k]) for k, (a, b) in enumerate(pairs)]
    for c in loads:
        c.start()

    bar = pltpu.get_barrier_semaphore()

    def hello(**where):
        pl.semaphore_signal(bar, inc=1, device_id=where, device_id_type=MESH)

    @pl.when(tile > 0)
    def _():
        hello(tile=tile - 1)

    @pl.when(tile < tiles - 1)
    def _():
        hello(tile=tile + 1)

    for p in x_peers:
        hello(lev=p)

    @pl.when(half == 0)
    def _():
        hello(lev=lev + 4)

    @pl.when(is_wrap)
    def _():
        for g in range(1, 4):

            @pl.when(g > order)
            def _():
                for k in range(4):
                    hello(**group(g, k))

    @pl.when(is_target)
    def _():
        def body(k, _):
            for j in (0, 4):
                hello(comp=comp - 2, tile=lax.rem(tile + k, tiles), lev=j)
            return 0

        lax.fori_loop(0, tiles, body, 0)

    lane = iota((16, 128), 1)

    blank = jnp.zeros((16, 640), F32)
    for k in range(3):
        ext[k] = blank
    for c in loads[:3]:
        c.wait()
    for k, ref in enumerate((t40, u40, d40)):
        for c in range(4):
            ext[k, 0:10, c * 128 : (c + 1) * 128] = ref[pl.ds(c, 10, stride=4), :]
    ends = [ext[k, :, 384:512] for k in range(3)]
    starts = [ext[k, :, 0:128] for k in range(3)]
    sendA[0] = jnp.where(
        lane >= 124, ends[0], jnp.where(lane >= 120, pltpu.roll(ends[1], 124, 1), pltpu.roll(ends[2], 120, 1))
    )
    sendA[1] = jnp.where(
        lane < 4, starts[0], jnp.where(lane < 8, pltpu.roll(starts[1], 4, 1), pltpu.roll(starts[2], 8, 1))
    )
    loads[3].wait()
    lane40 = iota((40, 128), 1)
    low40 = lane40 < 64
    zero40 = jnp.zeros((40, 128), F32)

    def pack(r, carry):
        to_right, to_left = carry
        mine = jnp.logical_and(lane40 >= 2 * r, lane40 < 2 * r + 2)
        to_right = jnp.where(mine, pltpu.roll(qin[r, :, 384:512], 2 * r + 2, 1), to_right)
        to_left = jnp.where(mine, pltpu.roll(qin[r, :, 0:128], 2 * r, 1), to_left)
        return to_right, to_left

    to_right, to_left = lax.fori_loop(0, 10, pack, (zero40, zero40))
    sendB[0] = to_right
    sendB[1] = to_left

    @pl.when(first)
    def _():
        haloA[0] = jnp.zeros((16, 128), F32)
        haloB[0] = zero40

    @pl.when(last)
    def _():
        haloA[1] = jnp.zeros((16, 128), F32)
        haloB[1] = zero40

    greeted = (
        jnp.where(tile > 0, 1, 0) + jnp.where(tile < tiles - 1, 1, 0) + 3 + half
        + jnp.where(jnp.logical_and(is_sky, x == 0), tiles, 0) + jnp.where(is_wrap, 4 * order, 0)
    )
    pl.semaphore_wait(bar, greeted)

    @pl.when(tile < tiles - 1)
    def _():
        send(sendA.at[0], haloA.at[0], sA.at[0], rA.at[0], tile=tile + 1)
        send(sendB.at[0], haloB.at[0], sB.at[0], rB.at[0], tile=tile + 1)

    @pl.when(tile > 0)
    def _():
        send(sendA.at[1], haloA.at[1], sA.at[1], rA.at[1], tile=tile - 1)
        send(sendB.at[1], haloB.at[1], sB.at[1], rB.at[1], tile=tile - 1)

    @pl.when(half == 1)
    def _():
        pl.semaphore_signal(ready, inc=1, device_id={"lev": lev - 4}, device_id_type=MESH)

    loads[4].wait()
    i, j = iota((48, 80), 0), iota((48, 80), 1)
    wanted = jnp.where(i < 16, lev * 10 + i, jnp.where(i < 32, other * 10 + i - 16, i - 32))
    used = jnp.where(i < 16, i, jnp.where(i < 32, i - 16, i - 23)) < 10
    pick_rows = jnp.where(jnp.logical_and(used, wanted == j), 1.0, 0.0).astype(F32)

    def pick_cols(count, start):
        i, j = iota((80, count), 0), iota((80, count), 1)
        r = lax.rem(j, 16)
        return jnp.where(jnp.logical_and(r < 10, i == start + (j // 16) * 10 + r), 1.0, 0.0).astype(F32)

    @pl.when(is_wrap)
    def _():
        edge = jnp.where(last, sendA[0], sendA[1])
        q3 = pltpu.roll(jnp.where(last, qin[0, 0:8, 384:512], qin[0, 0:8, 0:128]), 2, 0)
        ring[order, x, 0:8] = edge[0:8]
        ring[order, x, 8:16] = jnp.where(iota((8, 128), 0) < 2, edge[8:16], q3)
        mine = ring.at[order, x]
        for p in x_peers:
            send(mine, mine, sE.at[order], rE.at[order], lev=p)
        for g in range(0, 3):

            @pl.when(g < order)
            def _():
                for k in range(4):
                    send(mine, mine, sE.at[g], rE.at[order], **group(g, k))

        @pl.when(last)
        def _():
            send(sendB.at[0], wrapB, sW, rW, tile=0)

    picked = dot(pick_rows, m_v[...])
    matrix = dot(picked, pick_cols(64, half * 40))

    @pl.when(is_wrap)
    def _():
        mixed_rows[...] = dot(picked[0:16], pick_cols(128, 0))


    @pl.when(tile > 0)
    def _():
        drain(haloA.at[0], rA.at[0])
        drain(haloB.at[0], rB.at[0])

    @pl.when(tile < tiles - 1)
    def _():
        drain(haloA.at[1], rA.at[1])
        drain(haloB.at[1], rB.at[1])

    for k, block in enumerate(joined(haloA[1], haloA[0])):
        ext[k, :, 512:640] = block
    sky = jnp.where(is_sky, 1.0, 0.0).astype(F32)
    up, un = courant(ext[1])
    coef[0] = up
    coef[1] = un
    coef[2] = up * sky
    coef[3] = un * sky
    heat = heat_step(ext[0], up, un, ext[2])
    heat = heat_step(heat, up * sky, un * sky, ext[2] * sky)[:, 0:512]

    def level(r):
        edge = jnp.where(
            low40,
            pltpu.roll(haloB[1], lax.rem(128 - 2 * r, 128), 1),
            pltpu.roll(haloB[0], 126 - 2 * r, 1),
        )
        q = jnp.concatenate([qin[r], edge], axis=1)
        up, un, up2, un2 = (jnp.broadcast_to(coef[k, pl.ds(r, 1), :], (40, 640)) for k in range(4))
        q = tracer_step(tracer_step(q, up, un), up2, un2)
        qout[r] = q[:, 0:512]

    level(0)
    row8 = iota((8, 512), 0)
    rows_q = pltpu.roll(qout[0, 0:8, :], 2, 0)
    gath[x, 0:8, :] = heat[0:8]
    gath[x, 8:16, :] = jnp.where(row8 < 2, heat[8:16], jnp.where(row8 < 5, rows_q, 0.0))
    for k in range(3):
        send(gath.at[x], gath.at[x], sX.at[k], rX.at[k], lev=x_peers[k])
    for k in range(3):
        drain(gath.at[k], rX.at[k])
    product = dot(matrix, jnp.concatenate([gath[k] for k in range(4)], axis=0))
    top = product[32:33, :]

    @pl.when(jnp.logical_and(is_sky, half == 1))
    def _():
        piece[...] = jnp.where(
            x == 0, top[:, 0:128], jnp.where(x == 1, top[:, 128:256], jnp.where(x == 2, top[:, 256:384], top[:, 384:512]))
        )

        def body(k, _):
            send(piece, pieces.at[x, tile], sP, rP, comp=comp + 2, tile=k, lev=0)
            return 0

        lax.fori_loop(0, tiles, body, 0)

    @pl.when(jnp.logical_and(is_sky, half == 0))
    def _():
        line = jnp.where(
            x == 0, gath[0, 10:11, :], jnp.where(x == 1, gath[0, 11:12, :], jnp.where(x == 2, gath[0, 12:13, :], top))
        )
        for c in range(4):
            srow[c : c + 1, :] = line[:, c * 128 : (c + 1) * 128]

        def body(k, _):
            send(srow, rows.at[x, tile], sR, rR, comp=comp + 2, tile=lax.rem(tile + k, tiles), lev=0)
            return 0

        lax.fori_loop(0, tiles, body, 0)

    own[...] = product[0:16]
    for c in range(4):
        flip_s[pl.ds(c, 10, stride=4), :] = product[16:26, c * 128 : (c + 1) * 128]

    @pl.when(half == 1)
    def _():
        send(flip_s, flip_r, sF, rF, lev=other)

    def edge_heat(from_right, from_left, again):
        t, u, d = joined(from_right, from_left)
        up, un = courant(u)
        return heat_step(heat_step(t, up, un, d), up * again, un * again, d * again)

    def answer_later_ones(mine_order):
        mine = ring.at[mine_order, x]
        for g in range(mine_order + 1, 4):
            drain(ring.at[g], rE.at[g])
            for k in range(4):
                send(mine, mine, sE.at[g], rE.at[mine_order], **group(g, k))
            if mine_order % 2 == 0 and g == mine_order + 1:
                send(sendB.at[1], wrapB, sW, rW, tile=tiles - 1)

    def mix_edges(mine_order):
        drain(ring.at[mine_order, pl.ds(0, 3)], rE.at[mine_order])
        for g in range(mine_order):
            drain(ring.at[g], rE.at[g])
        stepped = [edge_heat(ring[2 * (k // 4), k % 4], ring[2 * (k // 4) + 1, k % 4], sky) for k in range(8)]
        mixed_v[...] = dot(mixed_rows[...], jnp.concatenate(stepped, axis=0))

    @pl.when(jnp.logical_and(first, half == 0))
    def _():
        answer_later_ones(0)
        mix_edges(0)

        @pl.when(jnp.logical_and(is_sky, lev == 0))
        def _():
            q, u, _ = joined(ring[0, 0], ring[1, 0])
            up, un = courant(jnp.broadcast_to(u[0:1], (8, 128)))
            edge_s[...] = tracer_step(tracer_step(q[8:16], up, un), up, un)
            edge_s[0:1, :] = mixed_v[0:1, :]

            def body(k, _):
                send(edge_s, edge_rows, sG, rG, comp=comp + 2, tile=k, lev=0)
                return 0

            lax.fori_loop(0, tiles, body, 0)

    def more(r, _):
        level(r)
        return 0

    lax.fori_loop(1, 10, more, 0)

    @pl.when(half == 0)
    def _():
        pl.semaphore_wait(ready, 1)
        send(flip_s, flip_r, sF, rF, lev=other)

    for c in loads[5:]:
        c.wait()

    for g in range(1, 4):

        @pl.when(jnp.logical_and(is_wrap, order == g))
        def _():
            answer_later_ones(g)
            mix_edges(g)

    @pl.when(is_wrap)
    def _():
        drain(wrapB, rW)
        up, un = courant(joined(ring[half * 2, x], ring[half * 2 + 1, x])[1])
        ring_coef[0] = up
        ring_coef[1] = un
        ring_coef[2] = up * sky
        ring_coef[3] = un * sky
        for flag, c, turn in ((first, 0, 126), (last, 3, 128)):

            @pl.when(flag)
            def _():
                def fix(r, _):
                    at = slice(c * 128, (c + 1) * 128)
                    far = pltpu.roll(wrapB[...], lax.rem(turn - 2 * r, 128), 1)
                    q = jnp.where(low40, qin[r, :, at], far) if c == 0 else jnp.where(low40, far, qin[r, :, at])
                    up, un, up2, un2 = (
                        jnp.broadcast_to(ring_coef[k, pl.ds(r, 1), :], (40, 128)) for k in range(4)
                    )
                    q = tracer_step(tracer_step(q, up, un), up2, un2)
                    new = lane40 < 2 if c == 0 else lane40 >= 126
                    qout[r, :, at] = jnp.where(new, q, qout[r, :, at])
                    return 0

                lax.fori_loop(0, 10, fix, 0)

    block = lax.shift_right_logical(i_s[0, 256], 9)
    before, after = lax.rem(block + tiles - 1, tiles), lax.rem(block + 1, tiles)
    lane1 = iota((1, 128), 1)

    def window(f):
        b, m, a = rows[f, before], rows[f, block], rows[f, after]
        w = [b[3:4]] + [m[c : c + 1] for c in range(4)] + [a[0:1]]
        if f == 3:
            extra = [pieces[3, before]] + [pieces[c, block] for c in range(4)] + [pieces[0, after]]
            w = [a + b for a, b in zip(w, extra)]
        edge = edge_rows[0:1, :] if f == 3 else edge_rows[2 + f : 3 + f, :]
        w[0] = jnp.where(lane1 >= jnp.where(before == tiles - 1, 126, 128), edge, w[0])
        w[1] = jnp.where(lane1 < jnp.where(block == 0, 2, 0), edge, w[1])
        w[4] = jnp.where(lane1 >= jnp.where(block == tiles - 1, 126, 128), edge, w[4])
        w[5] = jnp.where(lane1 < jnp.where(after == 0, 2, 0), edge, w[5])
        return w

    def remap(pair):
        windows = [window(f) for f in pair]
        for c in range(4):
            at = slice(c * 128, (c + 1) * 128)
            place = jnp.bitwise_and(i_v[:, at] - block * 512 + 128, tiles * 512 - 1)
            place = jnp.concatenate([place, place], axis=0)
            which, within = lax.shift_right_logical(place, 7), jnp.bitwise_and(place, 127)
            weight = w_v[:, at]
            sea = sea_v[c : c + 1, :] == 1
            got = jnp.zeros((8, 128), F32)
            for m in range(c, c + 3):
                source = jnp.concatenate([jnp.broadcast_to(w[m], (4, 128)) for w in windows], axis=0)
                taken = jnp.take_along_axis(source, within, axis=1, mode="promise_in_bounds")
                got = jnp.where(which == m, taken, got)
            for k, f in enumerate(pair):
                remapped = jnp.sum(got[4 * k : 4 * k + 4] * weight, axis=0, keepdims=True)
                if f < 3:
                    s = qout[0, f : f + 1, at]
                    qout[0, f : f + 1, at] = jnp.where(sea, s + 0.5 * (remapped - s), s)
                else:
                    s = tout[c : c + 1, :]
                    tout[c : c + 1, :] = jnp.where(sea, s + 0.5 * (remapped - s), s)

    @pl.when(is_target)
    def _():
        drain(edge_rows, rG)
        drain(rows, rR)
        remap((0, 1))

    drain(flip_r, rF)
    for c in range(4):
        tout[pl.ds(c, 10, stride=4), :] = own[0:10, c * 128 : (c + 1) * 128] + flip_r[pl.ds(c, 10, stride=4), :]

    @pl.when(is_wrap)
    def _():
        mixed = mixed_v[0:10, :]
        for flag, c, new in ((first, 0, lane < 2), (last, 3, lane >= 126)):

            @pl.when(flag)
            def _():
                tout[pl.ds(c, 10, stride=4), :] = jnp.where(new[0:10], mixed, tout[pl.ds(c, 10, stride=4), :])

    @pl.when(is_target)
    def _():
        drain(pieces, rP)
        remap((2, 3))

    @pl.when(tile < tiles - 1)
    def _():
        drain(sendA.at[0], sA.at[0])
        drain(sendB.at[0], sB.at[0])

    @pl.when(tile > 0)
    def _():
        drain(sendA.at[1], sA.at[1])
        drain(sendB.at[1], sB.at[1])

    for k in range(3):
        drain(gath.at[k], sX.at[k])
    drain(flip_s, sF)

    @pl.when(jnp.logical_and(is_sky, half == 0))
    def _():
        drain(rows.at[0], sR)

    @pl.when(jnp.logical_and(is_sky, half == 1))
    def _():
        drain(pieces.at[0], sP)

    @pl.when(is_wrap)
    def _():
        for g in range(4):

            @pl.when(g == order)
            def _():
                drain(ring.at[g, pl.ds(0, 3)], sE.at[g])

            @pl.when(g != order)
            def _():
                drain(ring.at[g], sE.at[g])

        drain(wrapB, sW)

        @pl.when(jnp.logical_and(is_sky, jnp.logical_and(first, lev == 0)))
        def _():
            drain(rows.at[0], sG)
            drain(rows.at[0], sG)


def body(t, u, q, d, m, w, i, sea):
    hbm = pl.BlockSpec(memory_space=pltpu.HBM)
    vmem = pl.BlockSpec(memory_space=pltpu.VMEM)
    dma = pltpu.SemaphoreType.DMA
    tiles = lax.axis_size("tile")
    buf = lambda *s: pltpu.VMEM(s, F32)
    tout, qout = pl.pallas_call(
        kernel,
        out_shape=(jax.ShapeDtypeStruct((40, 128), F32), jax.ShapeDtypeStruct((10, 40, 512), F32)),
        in_specs=[hbm] * 8,
        out_specs=(vmem, vmem),
        scratch_shapes=[
            buf(40, 128), buf(40, 128), buf(40, 128), buf(10, 40, 512), buf(80, 80),
            buf(4, 512), pltpu.VMEM((4, 512), jnp.int32), pltpu.SMEM((4, 512), jnp.int32), pltpu.VMEM((4, 128), jnp.int32),
            buf(3, 16, 640), buf(4, 16, 640), buf(2, 16, 128), buf(2, 40, 128), buf(2, 16, 128), buf(2, 40, 128),
            buf(4, 16, 512), buf(40, 128), buf(40, 128), buf(16, 512), buf(4, 128), buf(1, 128),
            buf(4, tiles, 4, 128), buf(4, tiles, 1, 128),
            buf(4, 4, 16, 128), buf(4, 16, 128), buf(40, 128), buf(8, 128), buf(8, 128), buf(16, 128), buf(16, 128),
            dma((9,)), dma((2,)), dma((2,)), dma((2,)), dma((2,)), dma((3,)), dma((3,)), dma, dma,
            dma, dma, dma, dma, dma((4,)), dma((4,)), dma, dma, dma, dma, pltpu.SemaphoreType.REGULAR,
        ],
        compiler_params=pltpu.CompilerParams(
            collective_id=0, has_side_effects=True, vmem_limit_bytes=24 * 1024 * 1024
        ),
    )(
        *(
            pltpu.with_memory_space_constraint(v, pltpu.HBM)
            for v in (
                t.reshape(40, 128), u.reshape(40, 128), d.reshape(40, 128), jnp.transpose(q[0], (1, 0, 2)),
                m[0], w.T, i.T, sea.reshape(4, 128),
            )
        )
    )
    return tout.reshape(1, 10, 512), jnp.transpose(qout, (1, 0, 2))[None]


def solution(mesh):
    in_specs = (
        P("comp", "lev", "tile"),
        P("comp", "lev", "tile"),
        P("comp", None, "lev", "tile"),
        P("comp", "lev", "tile"),
        P("comp", None, None),
        P("tile", None),
        P("tile", None),
        P("tile"),
    )
    out_specs = (P("comp", "lev", "tile"), P("comp", None, "lev", "tile"))
    return jax.shard_map(body, mesh=mesh, in_specs=in_specs, out_specs=out_specs, check_vma=False)
```

```python
import functools

import jax
import jax.numpy as jnp
from jax import lax
from jax.experimental import pallas as pl
from jax.experimental.pallas import tpu as pltpu
from jax.sharding import PartitionSpec as P

MESH = pl.DeviceIdType.MESH
F32 = jnp.float32
HIGHEST = lax.Precision.HIGHEST


def dot(a, b):
    return jnp.dot(a, b, precision=HIGHEST, preferred_element_type=F32)


def flux(q, up, un):
    n = q.shape[1]
    return up * q + un * pltpu.roll(q, n - 1, 1)


def tracer_step(q, up, un):
    f = flux(q, up, un)
    return q - (f - pltpu.roll(f, 1, 1))


def heat_step(t, up, un, d):
    n = t.shape[1]
    f = flux(t, up, un)
    return t + (
        -(f - pltpu.roll(f, 1, 1)) + d * (pltpu.roll(t, 1, 1) - 2.0 * t + pltpu.roll(t, n - 1, 1))
    )


def drain(ref, sem):
    pltpu.make_async_copy(ref, ref, sem).wait()


def send(src, dst, s, r, **where):
    pltpu.make_async_remote_copy(
        src_ref=src, dst_ref=dst, send_sem=s, recv_sem=r, device_id=where, device_id_type=MESH
    ).start()


def iota(shape, dim):
    return lax.broadcasted_iota(jnp.int32, shape, dim)


def joined(from_right, from_left):
    low = iota((16, 128), 1) < 64
    return (
        jnp.where(low, from_right, from_left),
        jnp.where(low, pltpu.roll(from_right, 124, 1), pltpu.roll(from_left, 4, 1)),
        jnp.where(low, pltpu.roll(from_right, 120, 1), pltpu.roll(from_left, 8, 1)),
    )


def courant(u):
    return jnp.maximum(u, 0.0), jnp.minimum(u, 0.0)


def kernel(
    t_hbm, u_hbm, d_hbm, q_hbm, m_hbm, w_hbm, i_hbm, sea_hbm,
    tout, qout,
    t40, u40, d40, qin, m_v, w_v, i_v, i_s, sea_v,
    ext, coef, sendA, sendB, haloA, haloB, gath, flip_s, flip_r, own, srow, piece, rows, pieces,
    ring, ring_coef, wrapB, edge_s, edge_rows, mixed_rows, mixed_v, relayB, answer, reply,
    in_sem, sA, rA, sB, rB, sX, rX, sF, rF, sR, rR, sP, rP, sE, rE, sW, rW, sG, rG, sV, rV, ready, go,
):
    comp, tile, lev = lax.axis_index("comp"), lax.axis_index("tile"), lax.axis_index("lev")
    tiles = lax.axis_size("tile")
    half, x = lev // 4, lax.rem(lev, 4)
    is_sky = comp < 2
    is_target = jnp.logical_and(comp >= 2, lev == 0)
    first, last = tile == 0, tile == tiles - 1
    is_wrap = jnp.logical_or(first, last)
    order = half * 2 + jnp.where(last, 1, 0)
    is_teller = jnp.logical_and(comp >= 2, x == 1)
    is_early = jnp.logical_and(half == 0, tile < tiles // 2)
    is_hub = jnp.logical_and(first, half == 0)
    x_peers = [half * 4 + lax.rem(x + k, 4) for k in range(1, 4)]
    other = lax.rem(lev + 4, 8)

    def group(g, k):
        return {"tile": (tiles - 1) * (g % 2), "lev": (g // 2) * 4 + k}

    pairs = (
        (t_hbm, t40), (u_hbm, u40), (d_hbm, d40), (q_hbm, qin), (m_hbm, m_v),
        (w_hbm, w_v), (i_hbm, i_v), (i_hbm, i_s), (sea_hbm, sea_v),
    )
    loads = [pltpu.make_async_copy(a, b, in_sem.at[k]) for k, (a, b) in enumerate(pairs)]
    for c in loads:
        c.start()

    bar = pltpu.get_barrier_semaphore()

    def hello(**where):
        pl.semaphore_signal(bar, inc=1, device_id=where, device_id_type=MESH)

    @pl.when(tile > 0)
    def _():
        hello(tile=tile - 1)

    @pl.when(tile < tiles - 1)
    def _():
        hello(tile=tile + 1)

    for p in x_peers:
        hello(lev=p)

    @pl.when(half == 0)
    def _():
        hello(lev=lev + 4)

    @pl.when(is_sky)
    def _():
        hello(comp=comp + 2, lev=half * 4 + 1)

    @pl.when(is_hub)
    def _():
        for g in range(1, 4):
            for k in range(4):
                hello(**group(g, k))

    @pl.when(is_target)
    def _():
        def body(k, _):
            for j in (1, 5):

                @pl.when(jnp.logical_or(k > 0, j > 1))
                def _():
                    hello(tile=lax.rem(tile + k, tiles), lev=j)

            return 0

        lax.fori_loop(0, tiles, body, 0)

    lane = iota((16, 128), 1)

    blank = jnp.zeros((16, 640), F32)
    for k in range(3):
        ext[k] = blank
    for c in loads[:3]:
        c.wait()
    for k, ref in enumerate((t40, u40, d40)):
        for c in range(4):
            ext[k, 0:10, c * 128 : (c + 1) * 128] = ref[pl.ds(c, 10, stride=4), :]
    ends = [ext[k, :, 384:512] for k in range(3)]
    starts = [ext[k, :, 0:128] for k in range(3)]
    sendA[0] = jnp.where(
        lane >= 124, ends[0], jnp.where(lane >= 120, pltpu.roll(ends[1], 124, 1), pltpu.roll(ends[2], 120, 1))
    )
    sendA[1] = jnp.where(
        lane < 4, starts[0], jnp.where(lane < 8, pltpu.roll(starts[1], 4, 1), pltpu.roll(starts[2], 8, 1))
    )
    loads[3].wait()
    lane40 = iota((40, 128), 1)
    low40 = lane40 < 64
    zero40 = jnp.zeros((40, 128), F32)

    def pack(r, carry):
        to_right, to_left = carry
        mine = jnp.logical_and(lane40 >= 2 * r, lane40 < 2 * r + 2)
        to_right = jnp.where(mine, pltpu.roll(qin[r, :, 384:512], 2 * r + 2, 1), to_right)
        to_left = jnp.where(mine, pltpu.roll(qin[r, :, 0:128], 2 * r, 1), to_left)
        return to_right, to_left

    to_right, to_left = lax.fori_loop(0, 10, pack, (zero40, zero40))
    sendB[0] = to_right
    sendB[1] = to_left

    @pl.when(first)
    def _():
        haloA[0] = jnp.zeros((16, 128), F32)
        haloB[0] = zero40

    @pl.when(last)
    def _():
        haloA[1] = jnp.zeros((16, 128), F32)
        haloB[1] = zero40

    greeted = (
        jnp.where(tile > 0, 1, 0) + jnp.where(tile < tiles - 1, 1, 0) + 3 + half
        + jnp.where(is_teller, tiles + 4 - jnp.where(half == 0, 1, 0), 0) + jnp.where(jnp.logical_and(is_wrap, order > 0), 4, 0)
    )
    pl.semaphore_wait(bar, greeted)

    @pl.when(tile < tiles - 1)
    def _():
        send(sendA.at[0], haloA.at[0], sA.at[0], rA.at[0], tile=tile + 1)
        send(sendB.at[0], haloB.at[0], sB.at[0], rB.at[0], tile=tile + 1)

    @pl.when(tile > 0)
    def _():
        send(sendA.at[1], haloA.at[1], sA.at[1], rA.at[1], tile=tile - 1)
        send(sendB.at[1], haloB.at[1], sB.at[1], rB.at[1], tile=tile - 1)

    @pl.when(half == 1)
    def _():
        pl.semaphore_signal(ready, inc=1, device_id={"lev": lev - 4}, device_id_type=MESH)

    @pl.when(is_teller)
    def _():
        for k in range(4):
            where = {"comp": comp - 2, "lev": half * 4 + k}
            pl.semaphore_signal(go, inc=1, device_id=where, device_id_type=MESH)

    loads[4].wait()
    i, j = iota((48, 80), 0), iota((48, 80), 1)
    wanted = jnp.where(i < 16, lev * 10 + i, jnp.where(i < 32, other * 10 + i - 16, i - 32))
    used = jnp.where(i < 16, i, jnp.where(i < 32, i - 16, i - 23)) < 10
    pick_rows = jnp.where(jnp.logical_and(used, wanted == j), 1.0, 0.0).astype(F32)

    def pick_cols(count, start):
        i, j = iota((80, count), 0), iota((80, count), 1)
        r = lax.rem(j, 16)
        return jnp.where(jnp.logical_and(r < 10, i == start + (j // 16) * 10 + r), 1.0, 0.0).astype(F32)

    @pl.when(is_wrap)
    def _():
        edge = jnp.where(last, sendA[0], sendA[1])
        q3 = pltpu.roll(jnp.where(last, qin[0, 0:8, 384:512], qin[0, 0:8, 0:128]), 2, 0)
        ring[order, x, 0:8] = edge[0:8]
        ring[order, x, 8:16] = jnp.where(iota((8, 128), 0) < 2, edge[8:16], q3)
        mine = ring.at[order, x]

        @pl.when(order == 0)
        def _():
            for p in x_peers:
                send(mine, mine, sE.at[0], rE.at[0], lev=p)

        @pl.when(order > 0)
        def _():
            for k in range(4):
                send(mine, mine, sE.at[0], rE.at[order], **group(0, k))

        @pl.when(order == 1)
        def _():
            send(sendB.at[0], wrapB, sW, rW, tile=0)

        @pl.when(order == 2)
        def _():
            send(sendB.at[1], relayB.at[0], sW, rV.at[0], tile=0, lev=x)

        @pl.when(order == 3)
        def _():
            send(sendB.at[0], relayB.at[1], sW, rV.at[1], tile=0, lev=x)

    picked = dot(pick_rows, m_v[...])
    matrix = dot(picked, pick_cols(64, half * 40))

    @pl.when(is_wrap)
    def _():
        mixed_rows[...] = dot(picked[0:32], pick_cols(128, 0))


    @pl.when(tile > 0)
    def _():
        drain(haloA.at[0], rA.at[0])
        drain(haloB.at[0], rB.at[0])

    @pl.when(tile < tiles - 1)
    def _():
        drain(haloA.at[1], rA.at[1])
        drain(haloB.at[1], rB.at[1])

    for k, block in enumerate(joined(haloA[1], haloA[0])):
        ext[k, :, 512:640] = block
    sky = jnp.where(is_sky, 1.0, 0.0).astype(F32)
    up, un = courant(ext[1])
    coef[0] = up
    coef[1] = un
    coef[2] = up * sky
    coef[3] = un * sky
    heat = heat_step(ext[0], up, un, ext[2])
    heat = heat_step(heat, up * sky, un * sky, ext[2] * sky)[:, 0:512]

    def level(r):
        edge = jnp.where(
            low40,
            pltpu.roll(haloB[1], lax.rem(128 - 2 * r, 128), 1),
            pltpu.roll(haloB[0], 126 - 2 * r, 1),
        )
        q = jnp.concatenate([qin[r], edge], axis=1)
        up, un, up2, un2 = (jnp.broadcast_to(coef[k, pl.ds(r, 1), :], (40, 640)) for k in range(4))
        q = tracer_step(tracer_step(q, up, un), up2, un2)
        qout[r] = q[:, 0:512]

    def tracers_inside():
        def more(r, _):
            level(r)
            return 0

        lax.fori_loop(1, 10, more, 0)

    level(0)
    row8 = iota((8, 512), 0)
    rows_q = pltpu.roll(qout[0, 0:8, :], 2, 0)
    gath[x, 0:8, :] = heat[0:8]
    gath[x, 8:16, :] = jnp.where(row8 < 2, heat[8:16], jnp.where(row8 < 5, rows_q, 0.0))
    for k in range(3):
        send(gath.at[x], gath.at[x], sX.at[k], rX.at[k], lev=x_peers[k])
    for k in range(3):
        drain(gath.at[k], rX.at[k])
    product = dot(matrix, jnp.concatenate([gath[k] for k in range(4)], axis=0))
    top = product[32:33, :]

    @pl.when(is_early)
    def _():
        tracers_inside()

    @pl.when(is_sky)
    def _():
        pl.semaphore_wait(go, 1)

    @pl.when(jnp.logical_and(is_sky, half == 1))
    def _():
        piece[...] = jnp.where(
            x == 0, top[:, 0:128], jnp.where(x == 1, top[:, 128:256], jnp.where(x == 2, top[:, 256:384], top[:, 384:512]))
        )

        def body(k, _):
            send(piece, pieces.at[x, tile], sP, rP, comp=comp + 2, tile=k, lev=0)
            return 0

        lax.fori_loop(0, tiles, body, 0)

    @pl.when(jnp.logical_and(is_sky, half == 0))
    def _():
        line = jnp.where(
            x == 0, gath[0, 10:11, :], jnp.where(x == 1, gath[0, 11:12, :], jnp.where(x == 2, gath[0, 12:13, :], top))
        )
        for c in range(4):
            srow[c : c + 1, :] = line[:, c * 128 : (c + 1) * 128]

        def body(k, _):
            send(srow, rows.at[x, tile], sR, rR, comp=comp + 2, tile=lax.rem(tile + k, tiles), lev=0)
            return 0

        lax.fori_loop(0, tiles, body, 0)

    own[...] = product[0:16]
    for c in range(4):
        flip_s[pl.ds(c, 10, stride=4), :] = product[16:26, c * 128 : (c + 1) * 128]

    @pl.when(half == 1)
    def _():
        send(flip_s, flip_r, sF, rF, lev=other)

    def edge_heat(from_right, from_left, again):
        t, u, d = joined(from_right, from_left)
        up, un = courant(u)
        return heat_step(heat_step(t, up, un, d), up * again, un * again, d * again)

    @pl.when(is_hub)
    def _():
        drain(ring.at[0, pl.ds(0, 3)], rE.at[0])
        for g in range(1, 4):
            drain(ring.at[g], rE.at[g])
        stepped = [edge_heat(ring[2 * (k // 4), k % 4], ring[2 * (k // 4) + 1, k % 4], sky) for k in range(8)]
        mixed = dot(mixed_rows[...], jnp.concatenate(stepped, axis=0))
        mixed_v[...] = mixed[0:16]

        @pl.when(jnp.logical_and(is_sky, lev == 0))
        def _():
            q, u, _ = joined(ring[0, 0], ring[1, 0])
            up, un = courant(jnp.broadcast_to(u[0:1], (8, 128)))
            edge_s[...] = tracer_step(tracer_step(q[8:16], up, un), up, un)
            edge_s[0:1, :] = mixed_v[0:1, :]

            def body(k, _):
                send(edge_s, edge_rows, sG, rG, comp=comp + 2, tile=k, lev=0)
                return 0

            lax.fori_loop(0, tiles, body, 0)

        answer[0, 0] = mixed[0:16]
        answer[1, 0] = mixed[16:32]
        answer[2, 0] = mixed[16:32]
        answer[0, 1] = ring[0, x]
        answer[1, 1] = ring[3, x]
        answer[2, 1] = ring[2, x]
        for g in range(1, 4):
            send(answer.at[g - 1], reply, sE.at[g], rE.at[0], **group(g, x))
        for k in range(2):
            drain(relayB.at[k], rV.at[k])
        for g, edge in ((1, sendB.at[1]), (2, relayB.at[1]), (3, relayB.at[0])):
            send(edge, wrapB, sV.at[g - 1], rW, **group(g, x))

    @pl.when(jnp.logical_not(is_early))
    def _():
        tracers_inside()

    @pl.when(half == 0)
    def _():
        pl.semaphore_wait(ready, 1)
        send(flip_s, flip_r, sF, rF, lev=other)

    for c in loads[5:]:
        c.wait()

    @pl.when(jnp.logical_and(is_wrap, order > 0))
    def _():
        drain(reply, rE.at[0])
        mixed_v[...] = reply[0]
        ring[half * 2 + jnp.where(last, 0, 1), x] = reply[1]

    @pl.when(is_wrap)
    def _():
        drain(wrapB, rW)
        up, un = courant(joined(ring[half * 2, x], ring[half * 2 + 1, x])[1])
        ring_coef[0] = up
        ring_coef[1] = un
        ring_coef[2] = up * sky
        ring_coef[3] = un * sky
        for flag, c, turn in ((first, 0, 126), (last, 3, 128)):

            @pl.when(flag)
            def _():
                def fix(r, _):
                    at = slice(c * 128, (c + 1) * 128)
                    far = pltpu.roll(wrapB[...], lax.rem(turn - 2 * r, 128), 1)
                    q = jnp.where(low40, qin[r, :, at], far) if c == 0 else jnp.where(low40, far, qin[r, :, at])
                    up, un, up2, un2 = (
                        jnp.broadcast_to(ring_coef[k, pl.ds(r, 1), :], (40, 128)) for k in range(4)
                    )
                    q = tracer_step(tracer_step(q, up, un), up2, un2)
                    new = lane40 < 2 if c == 0 else lane40 >= 126
                    qout[r, :, at] = jnp.where(new, q, qout[r, :, at])
                    return 0

                lax.fori_loop(0, 10, fix, 0)

    block = lax.shift_right_logical(i_s[0, 256], 9)
    before, after = lax.rem(block + tiles - 1, tiles), lax.rem(block + 1, tiles)
    lane1 = iota((1, 128), 1)

    def window(f):
        b, m, a = rows[f, before], rows[f, block], rows[f, after]
        w = [b[3:4]] + [m[c : c + 1] for c in range(4)] + [a[0:1]]
        if f == 3:
            extra = [pieces[3, before]] + [pieces[c, block] for c in range(4)] + [pieces[0, after]]
            w = [a + b for a, b in zip(w, extra)]
        edge = edge_rows[0:1, :] if f == 3 else edge_rows[2 + f : 3 + f, :]
        w[0] = jnp.where(lane1 >= jnp.where(before == tiles - 1, 126, 128), edge, w[0])
        w[1] = jnp.where(lane1 < jnp.where(block == 0, 2, 0), edge, w[1])
        w[4] = jnp.where(lane1 >= jnp.where(block == tiles - 1, 126, 128), edge, w[4])
        w[5] = jnp.where(lane1 < jnp.where(after == 0, 2, 0), edge, w[5])
        return w

    def remap(pair):
        windows = [window(f) for f in pair]
        for c in range(4):
            at = slice(c * 128, (c + 1) * 128)
            place = jnp.bitwise_and(i_v[:, at] - block * 512 + 128, tiles * 512 - 1)
            place = jnp.concatenate([place, place], axis=0)
            which, within = lax.shift_right_logical(place, 7), jnp.bitwise_and(place, 127)
            weight = w_v[:, at]
            sea = sea_v[c : c + 1, :] == 1
            got = jnp.zeros((8, 128), F32)
            for m in range(c, c + 3):
                source = jnp.concatenate([jnp.broadcast_to(w[m], (4, 128)) for w in windows], axis=0)
                taken = jnp.take_along_axis(source, within, axis=1, mode="promise_in_bounds")
                got = jnp.where(which == m, taken, got)
            for k, f in enumerate(pair):
                remapped = jnp.sum(got[4 * k : 4 * k + 4] * weight, axis=0, keepdims=True)
                if f < 3:
                    s = qout[0, f : f + 1, at]
                    qout[0, f : f + 1, at] = jnp.where(sea, s + 0.5 * (remapped - s), s)
                else:
                    s = tout[c : c + 1, :]
                    tout[c : c + 1, :] = jnp.where(sea, s + 0.5 * (remapped - s), s)

    @pl.when(is_target)
    def _():
        drain(edge_rows, rG)
        drain(rows, rR)
        remap((0, 1))

    drain(flip_r, rF)
    for c in range(4):
        tout[pl.ds(c, 10, stride=4), :] = own[0:10, c * 128 : (c + 1) * 128] + flip_r[pl.ds(c, 10, stride=4), :]

    @pl.when(is_wrap)
    def _():
        mixed = mixed_v[0:10, :]
        for flag, c, new in ((first, 0, lane < 2), (last, 3, lane >= 126)):

            @pl.when(flag)
            def _():
                tout[pl.ds(c, 10, stride=4), :] = jnp.where(new[0:10], mixed, tout[pl.ds(c, 10, stride=4), :])

    @pl.when(is_target)
    def _():
        drain(pieces, rP)
        remap((2, 3))

    @pl.when(tile < tiles - 1)
    def _():
        drain(sendA.at[0], sA.at[0])
        drain(sendB.at[0], sB.at[0])

    @pl.when(tile > 0)
    def _():
        drain(sendA.at[1], sA.at[1])
        drain(sendB.at[1], sB.at[1])

    for k in range(3):
        drain(gath.at[k], sX.at[k])
    drain(flip_s, sF)

    @pl.when(jnp.logical_and(is_sky, half == 0))
    def _():
        drain(rows.at[0], sR)

    @pl.when(jnp.logical_and(is_sky, half == 1))
    def _():
        drain(pieces.at[0], sP)

    @pl.when(is_wrap)
    def _():
        @pl.when(order > 0)
        def _():
            drain(ring.at[0], sE.at[0])
            drain(wrapB, sW)

        @pl.when(order == 0)
        def _():
            drain(ring.at[0, pl.ds(0, 3)], sE.at[0])
            for g in range(1, 4):
                drain(reply, sE.at[g])
                drain(wrapB, sV.at[g - 1])

        @pl.when(jnp.logical_and(is_sky, jnp.logical_and(first, lev == 0)))
        def _():
            drain(rows.at[0], sG)
            drain(rows.at[0], sG)


def body(t, u, q, d, m, w, i, sea):
    hbm = pl.BlockSpec(memory_space=pltpu.HBM)
    vmem = pl.BlockSpec(memory_space=pltpu.VMEM)
    dma = pltpu.SemaphoreType.DMA
    tiles = lax.axis_size("tile")
    buf = lambda *s: pltpu.VMEM(s, F32)
    tout, qout = pl.pallas_call(
        kernel,
        out_shape=(jax.ShapeDtypeStruct((40, 128), F32), jax.ShapeDtypeStruct((10, 40, 512), F32)),
        in_specs=[hbm] * 8,
        out_specs=(vmem, vmem),
        scratch_shapes=[
            buf(40, 128), buf(40, 128), buf(40, 128), buf(10, 40, 512), buf(80, 80),
            buf(4, 512), pltpu.VMEM((4, 512), jnp.int32), pltpu.SMEM((4, 512), jnp.int32), pltpu.VMEM((4, 128), jnp.int32),
            buf(3, 16, 640), buf(4, 16, 640), buf(2, 16, 128), buf(2, 40, 128), buf(2, 16, 128), buf(2, 40, 128),
            buf(4, 16, 512), buf(40, 128), buf(40, 128), buf(16, 512), buf(4, 128), buf(1, 128),
            buf(4, tiles, 4, 128), buf(4, tiles, 1, 128),
            buf(4, 4, 16, 128), buf(4, 16, 128), buf(40, 128), buf(8, 128), buf(8, 128), buf(32, 128), buf(16, 128),
            buf(2, 40, 128), buf(3, 2, 16, 128), buf(2, 16, 128),
            dma((9,)), dma((2,)), dma((2,)), dma((2,)), dma((2,)), dma((3,)), dma((3,)), dma, dma,
            dma, dma, dma, dma, dma((4,)), dma((4,)), dma, dma, dma, dma, dma((3,)), dma((2,)), pltpu.SemaphoreType.REGULAR, pltpu.SemaphoreType.REGULAR,
        ],
        compiler_params=pltpu.CompilerParams(
            collective_id=0, has_side_effects=True, vmem_limit_bytes=24 * 1024 * 1024
        ),
    )(
        *(
            pltpu.with_memory_space_constraint(v, pltpu.HBM)
            for v in (
                t.reshape(40, 128), u.reshape(40, 128), d.reshape(40, 128), jnp.transpose(q[0], (1, 0, 2)),
                m[0], w.T, i.T, sea.reshape(4, 128),
            )
        )
    )
    return tout.reshape(1, 10, 512), jnp.transpose(qout, (1, 0, 2))[None]


def solution(mesh):
    in_specs = (
        P("comp", "lev", "tile"),
        P("comp", "lev", "tile"),
        P("comp", None, "lev", "tile"),
        P("comp", "lev", "tile"),
        P("comp", None, None),
        P("tile", None),
        P("tile", None),
        P("tile"),
    )
    out_specs = (P("comp", "lev", "tile"), P("comp", None, "lev", "tile"))
    return jax.shard_map(body, mesh=mesh, in_specs=in_specs, out_specs=out_specs, check_vma=False)
```

```python
import functools

import jax
import jax.numpy as jnp
from jax import lax
from jax.experimental import pallas as pl
from jax.experimental.pallas import tpu as pltpu
from jax.sharding import PartitionSpec as P

MESH = pl.DeviceIdType.MESH
F32 = jnp.float32
HIGHEST = lax.Precision.HIGHEST


def dot(a, b):
    return jnp.dot(a, b, precision=HIGHEST, preferred_element_type=F32)


def flux(q, up, un):
    n = q.shape[1]
    return up * q + un * pltpu.roll(q, n - 1, 1)


def tracer_step(q, up, un):
    f = flux(q, up, un)
    return q - (f - pltpu.roll(f, 1, 1))


def heat_step(t, up, un, d):
    n = t.shape[1]
    f = flux(t, up, un)
    return t + (
        -(f - pltpu.roll(f, 1, 1)) + d * (pltpu.roll(t, 1, 1) - 2.0 * t + pltpu.roll(t, n - 1, 1))
    )


def drain(ref, sem):
    pltpu.make_async_copy(ref, ref, sem).wait()


def send(src, dst, s, r, **where):
    pltpu.make_async_remote_copy(
        src_ref=src, dst_ref=dst, send_sem=s, recv_sem=r, device_id=where, device_id_type=MESH
    ).start()


def iota(shape, dim):
    return lax.broadcasted_iota(jnp.int32, shape, dim)


def joined(from_right, from_left):
    low = iota((16, 128), 1) < 64
    return (
        jnp.where(low, from_right, from_left),
        jnp.where(low, pltpu.roll(from_right, 124, 1), pltpu.roll(from_left, 4, 1)),
        jnp.where(low, pltpu.roll(from_right, 120, 1), pltpu.roll(from_left, 8, 1)),
    )


def courant(u):
    return jnp.maximum(u, 0.0), jnp.minimum(u, 0.0)


def kernel(
    t_hbm, u_hbm, d_hbm, q_hbm, m_hbm, w_hbm, i_hbm, sea_hbm,
    tout, qout,
    t40, u40, d40, qin, m_v, w_v, i_v, i_s, sea_v,
    ext, coef, sendA, sendB, haloA, haloB, gath, flip_s, flip_r, own, srow, piece, rows, pieces,
    ring, ring_coef, wrapB, edge_s, edge_rows, mixed_rows, mixed_v, relayB, answer, reply, parts, landed,
    in_sem, sA, rA, sB, rB, sX, rX, sF, rF, sR, rR, sP, rP, sE, rE, sW, rW, sG, rG, sV, rV, sT, rT, ready, go,
):
    comp, tile, lev = lax.axis_index("comp"), lax.axis_index("tile"), lax.axis_index("lev")
    tiles = lax.axis_size("tile")
    half, x = lev // 4, lax.rem(lev, 4)
    is_sky = comp < 2
    is_target = jnp.logical_and(comp >= 2, lev == 0)
    first, last = tile == 0, tile == tiles - 1
    is_wrap = jnp.logical_or(first, last)
    order = half * 2 + jnp.where(last, 1, 0)
    is_teller = jnp.logical_and(comp >= 2, x == 1)
    is_late_sky = jnp.logical_and(is_sky, half == 1)
    is_early = jnp.logical_and(half == 0, tile < tiles // 2)
    is_hub = jnp.logical_and(first, half == 0)
    x_peers = [half * 4 + lax.rem(x + k, 4) for k in range(1, 4)]
    other = lax.rem(lev + 4, 8)

    def group(g, k):
        return {"tile": (tiles - 1) * (g % 2), "lev": (g // 2) * 4 + k}

    pairs = (
        (t_hbm, t40), (u_hbm, u40), (d_hbm, d40), (q_hbm, qin), (m_hbm, m_v),
        (w_hbm, w_v), (i_hbm, i_v), (i_hbm, i_s), (sea_hbm, sea_v),
    )
    loads = [pltpu.make_async_copy(a, b, in_sem.at[k]) for k, (a, b) in enumerate(pairs)]
    for c in loads:
        c.start()

    bar = pltpu.get_barrier_semaphore()

    def hello(**where):
        pl.semaphore_signal(bar, inc=1, device_id=where, device_id_type=MESH)

    @pl.when(tile > 0)
    def _():
        hello(tile=tile - 1)

    @pl.when(tile < tiles - 1)
    def _():
        hello(tile=tile + 1)

    for p in x_peers:
        hello(lev=p)

    @pl.when(half == 0)
    def _():
        hello(lev=lev + 4)

    @pl.when(is_sky)
    def _():
        hello(comp=comp + 2, lev=half * 4 + 1)

    @pl.when(is_hub)
    def _():
        for g in range(1, 4):
            for k in range(4):
                hello(**group(g, k))

    @pl.when(is_target)
    def _():
        def body(k, _):
            for j in (1, 5):

                @pl.when(jnp.logical_or(k > 0, j > 1))
                def _():
                    hello(tile=lax.rem(tile + k, tiles), lev=j)

            return 0

        lax.fori_loop(0, tiles, body, 0)

    lane = iota((16, 128), 1)

    blank = jnp.zeros((16, 640), F32)
    for k in range(3):
        ext[k] = blank
    for c in loads[:3]:
        c.wait()
    for k, ref in enumerate((t40, u40, d40)):
        for c in range(4):
            ext[k, 0:10, c * 128 : (c + 1) * 128] = ref[pl.ds(c, 10, stride=4), :]
    ends = [ext[k, :, 384:512] for k in range(3)]
    starts = [ext[k, :, 0:128] for k in range(3)]
    sendA[0] = jnp.where(
        lane >= 124, ends[0], jnp.where(lane >= 120, pltpu.roll(ends[1], 124, 1), pltpu.roll(ends[2], 120, 1))
    )
    sendA[1] = jnp.where(
        lane < 4, starts[0], jnp.where(lane < 8, pltpu.roll(starts[1], 4, 1), pltpu.roll(starts[2], 8, 1))
    )
    loads[3].wait()
    lane40 = iota((40, 128), 1)
    low40 = lane40 < 64
    zero40 = jnp.zeros((40, 128), F32)

    def pack(r, carry):
        to_right, to_left = carry
        mine = jnp.logical_and(lane40 >= 2 * r, lane40 < 2 * r + 2)
        to_right = jnp.where(mine, pltpu.roll(qin[r, :, 384:512], 2 * r + 2, 1), to_right)
        to_left = jnp.where(mine, pltpu.roll(qin[r, :, 0:128], 2 * r, 1), to_left)
        return to_right, to_left

    to_right, to_left = lax.fori_loop(0, 10, pack, (zero40, zero40))
    sendB[0] = to_right
    sendB[1] = to_left

    @pl.when(first)
    def _():
        haloA[0] = jnp.zeros((16, 128), F32)
        haloB[0] = zero40

    @pl.when(last)
    def _():
        haloA[1] = jnp.zeros((16, 128), F32)
        haloB[1] = zero40

    greeted = (
        jnp.where(tile > 0, 1, 0) + jnp.where(tile < tiles - 1, 1, 0) + 3 + half
        + jnp.where(is_teller, tiles + 4 - jnp.where(half == 0, 1, 0), 0) + jnp.where(jnp.logical_and(is_wrap, order > 0), 4, 0)
    )
    pl.semaphore_wait(bar, greeted)

    @pl.when(tile < tiles - 1)
    def _():
        send(sendA.at[0], haloA.at[0], sA.at[0], rA.at[0], tile=tile + 1)
        send(sendB.at[0], haloB.at[0], sB.at[0], rB.at[0], tile=tile + 1)

    @pl.when(tile > 0)
    def _():
        send(sendA.at[1], haloA.at[1], sA.at[1], rA.at[1], tile=tile - 1)
        send(sendB.at[1], haloB.at[1], sB.at[1], rB.at[1], tile=tile - 1)

    @pl.when(half == 1)
    def _():
        pl.semaphore_signal(ready, inc=1, device_id={"lev": lev - 4}, device_id_type=MESH)

    @pl.when(is_teller)
    def _():
        for k in range(4):
            where = {"comp": comp - 2, "lev": half * 4 + k}
            pl.semaphore_signal(go, inc=1, device_id=where, device_id_type=MESH)

    loads[4].wait()
    i, j = iota((48, 80), 0), iota((48, 80), 1)
    wanted = jnp.where(i < 16, lev * 10 + i, jnp.where(i < 32, other * 10 + i - 16, i - 32))
    used = jnp.where(i < 16, i, jnp.where(i < 32, i - 16, i - 23)) < 10
    pick_rows = jnp.where(jnp.logical_and(used, wanted == j), 1.0, 0.0).astype(F32)

    def pick_cols(count, start):
        i, j = iota((80, count), 0), iota((80, count), 1)
        r = lax.rem(j, 16)
        return jnp.where(jnp.logical_and(r < 10, i == start + (j // 16) * 10 + r), 1.0, 0.0).astype(F32)

    @pl.when(is_wrap)
    def _():
        edge = jnp.where(last, sendA[0], sendA[1])
        q3 = pltpu.roll(jnp.where(last, qin[0, 0:8, 384:512], qin[0, 0:8, 0:128]), 2, 0)
        ring[order, x, 0:8] = edge[0:8]
        ring[order, x, 8:16] = jnp.where(iota((8, 128), 0) < 2, edge[8:16], q3)
        mine = ring.at[order, x]

        @pl.when(order == 0)
        def _():
            for p in x_peers:
                send(mine, mine, sE.at[0], rE.at[0], lev=p)

        @pl.when(order > 0)
        def _():
            for k in range(4):
                send(mine, mine, sE.at[0], rE.at[order], **group(0, k))

        @pl.when(order == 1)
        def _():
            send(sendB.at[0], wrapB, sW, rW, tile=0)

        @pl.when(order == 2)
        def _():
            send(sendB.at[1], relayB.at[0], sW, rV.at[0], tile=0, lev=x)

        @pl.when(order == 3)
        def _():
            send(sendB.at[0], relayB.at[1], sW, rV.at[1], tile=0, lev=x)

    here = jnp.logical_and(iota((16, 80), 0) < 10, iota((16, 80), 1) == lev * 10 + iota((16, 80), 0))
    top_row = jnp.broadcast_to(m_v[0:1, :], (16, 80))
    scale = jnp.sum(jnp.where(here, top_row, 0.0), axis=1, keepdims=True)
    picked = dot(pick_rows, m_v[...])
    matrix = dot(picked, pick_cols(64, half * 40))

    @pl.when(is_wrap)
    def _():
        mixed_rows[...] = dot(picked[0:32], pick_cols(128, 0))


    @pl.when(tile > 0)
    def _():
        drain(haloA.at[0], rA.at[0])

    @pl.when(tile < tiles - 1)
    def _():
        drain(haloA.at[1], rA.at[1])

    for k, block in enumerate(joined(haloA[1], haloA[0])):
        ext[k, :, 512:640] = block
    sky = jnp.where(is_sky, 1.0, 0.0).astype(F32)
    up, un = courant(ext[1])
    coef[0] = up
    coef[1] = un
    coef[2] = up * sky
    coef[3] = un * sky
    heat = heat_step(ext[0], up, un, ext[2])
    heat = heat_step(heat, up * sky, un * sky, ext[2] * sky)[:, 0:512]

    @pl.when(is_late_sky)
    def _():
        part = jnp.sum(heat * scale, axis=0, keepdims=True)
        for c in range(4):
            parts[c] = part[:, c * 128 : (c + 1) * 128]
        landed[x] = parts[x]
        for k in range(3):
            send(parts.at[lax.rem(x + k + 1, 4)], landed.at[x], sT.at[k], rT.at[k], lev=x_peers[k])

    def level(r):
        edge = jnp.where(
            low40,
            pltpu.roll(haloB[1], lax.rem(128 - 2 * r, 128), 1),
            pltpu.roll(haloB[0], 126 - 2 * r, 1),
        )
        q = jnp.concatenate([qin[r], edge], axis=1)
        up, un, up2, un2 = (jnp.broadcast_to(coef[k, pl.ds(r, 1), :], (40, 640)) for k in range(4))
        q = tracer_step(tracer_step(q, up, un), up2, un2)
        qout[r] = q[:, 0:512]

    def tracers_inside():
        def more(r, _):
            level(r)
            return 0

        lax.fori_loop(1, 10, more, 0)

    row8 = iota((8, 512), 0)
    gath[x, 0:8, :] = heat[0:8]
    gath[x, 8:16, :] = jnp.where(row8 < 2, heat[8:16], 0.0)

    def share():
        for k in range(3):
            send(gath.at[x], gath.at[x], sX.at[k], rX.at[k], lev=x_peers[k])

    @pl.when(half == 1)
    def _():
        share()

    @pl.when(tile > 0)
    def _():
        drain(haloB.at[0], rB.at[0])

    @pl.when(tile < tiles - 1)
    def _():
        drain(haloB.at[1], rB.at[1])

    level(0)

    @pl.when(half == 0)
    def _():
        rows_q = pltpu.roll(qout[0, 0:8, :], 2, 0)
        gath[x, 8:16, :] = jnp.where(row8 < 2, heat[8:16], jnp.where(row8 < 5, rows_q, 0.0))
        share()

    def late_rows(start, stop):
        def body(k, _):
            send(piece, pieces.at[x, tile], sP, rP, comp=comp + 2, tile=k, lev=0)
            return 0

        lax.fori_loop(start, stop, body, 0)

    @pl.when(is_late_sky)
    def _():
        for k in range(3):
            drain(landed.at[k], rT.at[k])
        piece[...] = landed[0] + landed[1] + landed[2] + landed[3]
        pl.semaphore_wait(go, 1)
        late_rows(0, 8)

    for k in range(3):
        drain(gath.at[k], rX.at[k])
    product = dot(matrix, jnp.concatenate([gath[k] for k in range(4)], axis=0))
    top = product[32:33, :]

    @pl.when(is_early)
    def _():
        tracers_inside()

    @pl.when(jnp.logical_and(is_sky, half == 0))
    def _():
        pl.semaphore_wait(go, 1)
        line = jnp.where(
            x == 0, gath[0, 10:11, :], jnp.where(x == 1, gath[0, 11:12, :], jnp.where(x == 2, gath[0, 12:13, :], top))
        )
        for c in range(4):
            srow[c : c + 1, :] = line[:, c * 128 : (c + 1) * 128]

        def body(k, _):
            send(srow, rows.at[x, tile], sR, rR, comp=comp + 2, tile=lax.rem(tile + k, tiles), lev=0)
            return 0

        lax.fori_loop(0, tiles, body, 0)

    own[...] = product[0:16]
    for c in range(4):
        flip_s[pl.ds(c, 10, stride=4), :] = product[16:26, c * 128 : (c + 1) * 128]

    @pl.when(half == 1)
    def _():
        send(flip_s, flip_r, sF, rF, lev=other)

    @pl.when(is_late_sky)
    def _():
        late_rows(8, tiles)

    def edge_heat(from_right, from_left, again):
        t, u, d = joined(from_right, from_left)
        up, un = courant(u)
        return heat_step(heat_step(t, up, un, d), up * again, un * again, d * again)

    @pl.when(is_hub)
    def _():
        drain(ring.at[0, pl.ds(0, 3)], rE.at[0])
        for g in range(1, 4):
            drain(ring.at[g], rE.at[g])
        stepped = [edge_heat(ring[2 * (k // 4), k % 4], ring[2 * (k // 4) + 1, k % 4], sky) for k in range(8)]
        mixed = dot(mixed_rows[...], jnp.concatenate(stepped, axis=0))
        mixed_v[...] = mixed[0:16]

        @pl.when(jnp.logical_and(is_sky, lev == 0))
        def _():
            q, u, _ = joined(ring[0, 0], ring[1, 0])
            up, un = courant(jnp.broadcast_to(u[0:1], (8, 128)))
            edge_s[...] = tracer_step(tracer_step(q[8:16], up, un), up, un)
            edge_s[0:1, :] = mixed_v[0:1, :]

            def body(k, _):
                send(edge_s, edge_rows, sG, rG, comp=comp + 2, tile=k, lev=0)
                return 0

            lax.fori_loop(0, tiles, body, 0)

        answer[0, 0] = mixed[0:16]
        answer[1, 0] = mixed[16:32]
        answer[2, 0] = mixed[16:32]
        answer[0, 1] = ring[0, x]
        answer[1, 1] = ring[3, x]
        answer[2, 1] = ring[2, x]
        for g in range(1, 4):
            send(answer.at[g - 1], reply, sE.at[g], rE.at[0], **group(g, x))
        for k in range(2):
            drain(relayB.at[k], rV.at[k])
        for g, edge in ((1, sendB.at[1]), (2, relayB.at[1]), (3, relayB.at[0])):
            send(edge, wrapB, sV.at[g - 1], rW, **group(g, x))

    @pl.when(jnp.logical_not(is_early))
    def _():
        tracers_inside()

    @pl.when(half == 0)
    def _():
        pl.semaphore_wait(ready, 1)
        send(flip_s, flip_r, sF, rF, lev=other)

    for c in loads[5:]:
        c.wait()

    @pl.when(jnp.logical_and(is_wrap, order > 0))
    def _():
        drain(reply, rE.at[0])
        mixed_v[...] = reply[0]
        ring[half * 2 + jnp.where(last, 0, 1), x] = reply[1]

    @pl.when(is_wrap)
    def _():
        drain(wrapB, rW)
        up, un = courant(joined(ring[half * 2, x], ring[half * 2 + 1, x])[1])
        ring_coef[0] = up
        ring_coef[1] = un
        ring_coef[2] = up * sky
        ring_coef[3] = un * sky
        for flag, c, turn in ((first, 0, 126), (last, 3, 128)):

            @pl.when(flag)
            def _():
                def fix(r, _):
                    at = slice(c * 128, (c + 1) * 128)
                    far = pltpu.roll(wrapB[...], lax.rem(turn - 2 * r, 128), 1)
                    q = jnp.where(low40, qin[r, :, at], far) if c == 0 else jnp.where(low40, far, qin[r, :, at])
                    up, un, up2, un2 = (
                        jnp.broadcast_to(ring_coef[k, pl.ds(r, 1), :], (40, 128)) for k in range(4)
                    )
                    q = tracer_step(tracer_step(q, up, un), up2, un2)
                    new = lane40 < 2 if c == 0 else lane40 >= 126
                    qout[r, :, at] = jnp.where(new, q, qout[r, :, at])
                    return 0

                lax.fori_loop(0, 10, fix, 0)

    block = lax.shift_right_logical(i_s[0, 256], 9)
    before, after = lax.rem(block + tiles - 1, tiles), lax.rem(block + 1, tiles)
    lane1 = iota((1, 128), 1)

    def window(f):
        b, m, a = rows[f, before], rows[f, block], rows[f, after]
        w = [b[3:4]] + [m[c : c + 1] for c in range(4)] + [a[0:1]]
        if f == 3:
            extra = [pieces[3, before]] + [pieces[c, block] for c in range(4)] + [pieces[0, after]]
            w = [a + b for a, b in zip(w, extra)]
        edge = edge_rows[0:1, :] if f == 3 else edge_rows[2 + f : 3 + f, :]
        w[0] = jnp.where(lane1 >= jnp.where(before == tiles - 1, 126, 128), edge, w[0])
        w[1] = jnp.where(lane1 < jnp.where(block == 0, 2, 0), edge, w[1])
        w[4] = jnp.where(lane1 >= jnp.where(block == tiles - 1, 126, 128), edge, w[4])
        w[5] = jnp.where(lane1 < jnp.where(after == 0, 2, 0), edge, w[5])
        return w

    def remap(pair):
        windows = [window(f) for f in pair]
        for c in range(4):
            at = slice(c * 128, (c + 1) * 128)
            place = jnp.bitwise_and(i_v[:, at] - block * 512 + 128, tiles * 512 - 1)
            place = jnp.concatenate([place, place], axis=0)
            which, within = lax.shift_right_logical(place, 7), jnp.bitwise_and(place, 127)
            weight = w_v[:, at]
            sea = sea_v[c : c + 1, :] == 1
            got = jnp.zeros((8, 128), F32)
            for m in range(c, c + 3):
                source = jnp.concatenate([jnp.broadcast_to(w[m], (4, 128)) for w in windows], axis=0)
                taken = jnp.take_along_axis(source, within, axis=1, mode="promise_in_bounds")
                got = jnp.where(which == m, taken, got)
            for k, f in enumerate(pair):
                remapped = jnp.sum(got[4 * k : 4 * k + 4] * weight, axis=0, keepdims=True)
                if f < 3:
                    s = qout[0, f : f + 1, at]
                    qout[0, f : f + 1, at] = jnp.where(sea, s + 0.5 * (remapped - s), s)
                else:
                    s = tout[c : c + 1, :]
                    tout[c : c + 1, :] = jnp.where(sea, s + 0.5 * (remapped - s), s)

    @pl.when(is_target)
    def _():
        drain(edge_rows, rG)
        drain(rows, rR)
        remap((0, 1))

    drain(flip_r, rF)
    for c in range(4):
        tout[pl.ds(c, 10, stride=4), :] = own[0:10, c * 128 : (c + 1) * 128] + flip_r[pl.ds(c, 10, stride=4), :]

    @pl.when(is_wrap)
    def _():
        mixed = mixed_v[0:10, :]
        for flag, c, new in ((first, 0, lane < 2), (last, 3, lane >= 126)):

            @pl.when(flag)
            def _():
                tout[pl.ds(c, 10, stride=4), :] = jnp.where(new[0:10], mixed, tout[pl.ds(c, 10, stride=4), :])

    @pl.when(is_target)
    def _():
        drain(pieces, rP)
        remap((2, 3))

    @pl.when(tile < tiles - 1)
    def _():
        drain(sendA.at[0], sA.at[0])
        drain(sendB.at[0], sB.at[0])

    @pl.when(tile > 0)
    def _():
        drain(sendA.at[1], sA.at[1])
        drain(sendB.at[1], sB.at[1])

    for k in range(3):
        drain(gath.at[k], sX.at[k])
    drain(flip_s, sF)

    @pl.when(jnp.logical_and(is_sky, half == 0))
    def _():
        drain(rows.at[0], sR)

    @pl.when(jnp.logical_and(is_sky, half == 1))
    def _():
        drain(pieces.at[0], sP)
        for k in range(3):
            drain(parts.at[k], sT.at[k])

    @pl.when(is_wrap)
    def _():
        @pl.when(order > 0)
        def _():
            drain(ring.at[0], sE.at[0])
            drain(wrapB, sW)

        @pl.when(order == 0)
        def _():
            drain(ring.at[0, pl.ds(0, 3)], sE.at[0])
            for g in range(1, 4):
                drain(reply, sE.at[g])
                drain(wrapB, sV.at[g - 1])

        @pl.when(jnp.logical_and(is_sky, jnp.logical_and(first, lev == 0)))
        def _():
            drain(rows.at[0], sG)
            drain(rows.at[0], sG)


def body(t, u, q, d, m, w, i, sea):
    hbm = pl.BlockSpec(memory_space=pltpu.HBM)
    vmem = pl.BlockSpec(memory_space=pltpu.VMEM)
    dma = pltpu.SemaphoreType.DMA
    tiles = lax.axis_size("tile")
    buf = lambda *s: pltpu.VMEM(s, F32)
    tout, qout = pl.pallas_call(
        kernel,
        out_shape=(jax.ShapeDtypeStruct((40, 128), F32), jax.ShapeDtypeStruct((10, 40, 512), F32)),
        in_specs=[hbm] * 8,
        out_specs=(vmem, vmem),
        scratch_shapes=[
            buf(40, 128), buf(40, 128), buf(40, 128), buf(10, 40, 512), buf(80, 80),
            buf(4, 512), pltpu.VMEM((4, 512), jnp.int32), pltpu.SMEM((4, 512), jnp.int32), pltpu.VMEM((4, 128), jnp.int32),
            buf(3, 16, 640), buf(4, 16, 640), buf(2, 16, 128), buf(2, 40, 128), buf(2, 16, 128), buf(2, 40, 128),
            buf(4, 16, 512), buf(40, 128), buf(40, 128), buf(16, 512), buf(4, 128), buf(1, 128),
            buf(4, tiles, 4, 128), buf(4, tiles, 1, 128),
            buf(4, 4, 16, 128), buf(4, 16, 128), buf(40, 128), buf(8, 128), buf(8, 128), buf(32, 128), buf(16, 128),
            buf(2, 40, 128), buf(3, 2, 16, 128), buf(2, 16, 128), buf(4, 1, 128), buf(4, 1, 128),
            dma((9,)), dma((2,)), dma((2,)), dma((2,)), dma((2,)), dma((3,)), dma((3,)), dma, dma,
            dma, dma, dma, dma, dma((4,)), dma((4,)), dma, dma, dma, dma, dma((3,)), dma((2,)), dma((3,)), dma((3,)), pltpu.SemaphoreType.REGULAR, pltpu.SemaphoreType.REGULAR,
        ],
        compiler_params=pltpu.CompilerParams(
            collective_id=0, has_side_effects=True, vmem_limit_bytes=24 * 1024 * 1024
        ),
    )(
        *(
            pltpu.with_memory_space_constraint(v, pltpu.HBM)
            for v in (
                t.reshape(40, 128), u.reshape(40, 128), d.reshape(40, 128), jnp.transpose(q[0], (1, 0, 2)),
                m[0], w.T, i.T, sea.reshape(4, 128),
            )
        )
    )
    return tout.reshape(1, 10, 512), jnp.transpose(qout, (1, 0, 2))[None]


def solution(mesh):
    in_specs = (
        P("comp", "lev", "tile"),
        P("comp", "lev", "tile"),
        P("comp", None, "lev", "tile"),
        P("comp", "lev", "tile"),
        P("comp", None, None),
        P("tile", None),
        P("tile", None),
        P("tile"),
    )
    out_specs = (P("comp", "lev", "tile"), P("comp", None, "lev", "tile"))
    return jax.shard_map(body, mesh=mesh, in_specs=in_specs, out_specs=out_specs, check_vma=False)
```

```python
import functools

import jax
import jax.numpy as jnp
from jax import lax
from jax.experimental import pallas as pl
from jax.experimental.pallas import tpu as pltpu
from jax.sharding import PartitionSpec as P

MESH = pl.DeviceIdType.MESH
F32 = jnp.float32
HIGHEST = lax.Precision.HIGHEST


def dot(a, b):
    return jnp.dot(a, b, precision=HIGHEST, preferred_element_type=F32)


def flux(q, up, un):
    n = q.shape[1]
    return up * q + un * pltpu.roll(q, n - 1, 1)


def tracer_step(q, up, un):
    f = flux(q, up, un)
    return q - (f - pltpu.roll(f, 1, 1))


def heat_step(t, up, un, d):
    n = t.shape[1]
    f = flux(t, up, un)
    return t + (
        -(f - pltpu.roll(f, 1, 1)) + d * (pltpu.roll(t, 1, 1) - 2.0 * t + pltpu.roll(t, n - 1, 1))
    )


def drain(ref, sem):
    pltpu.make_async_copy(ref, ref, sem).wait()


def send(src, dst, s, r, **where):
    pltpu.make_async_remote_copy(
        src_ref=src, dst_ref=dst, send_sem=s, recv_sem=r, device_id=where, device_id_type=MESH
    ).start()


def iota(shape, dim):
    return lax.broadcasted_iota(jnp.int32, shape, dim)


def joined(from_right, from_left):
    low = iota((16, 128), 1) < 64
    return (
        jnp.where(low, from_right, from_left),
        jnp.where(low, pltpu.roll(from_right, 124, 1), pltpu.roll(from_left, 4, 1)),
        jnp.where(low, pltpu.roll(from_right, 120, 1), pltpu.roll(from_left, 8, 1)),
    )


def courant(u):
    return jnp.maximum(u, 0.0), jnp.minimum(u, 0.0)


def kernel(
    t_hbm, u_hbm, d_hbm, q_hbm, m_hbm, w_hbm, i_hbm, sea_hbm,
    tout, qout,
    t40, u40, d40, qin, m_v, w_v, i_v, i_s, sea_v,
    ext, coef, sendA, sendB, haloA, haloB, gath, flip_s, flip_r, own, srow, piece, rows, pieces,
    ring, ring_coef, wrapB, edge_s, edge_rows, mixed_rows, mixed_v, relayB, answer, reply, parts, landed,
    in_sem, sA, rA, sB, rB, sX, rX, sF, rF, sR, rR, sP, rP, sE, rE, sW, rW, sG, rG, sV, rV, sT, rT, ready, go, hub_up,
):
    comp, tile, lev = lax.axis_index("comp"), lax.axis_index("tile"), lax.axis_index("lev")
    tiles = lax.axis_size("tile")
    half, x = lev // 4, lax.rem(lev, 4)
    is_sky = comp < 2
    is_target = jnp.logical_and(comp >= 2, lev == 0)
    first, last = tile == 0, tile == tiles - 1
    is_wrap = jnp.logical_or(first, last)
    order = half * 2 + jnp.where(last, 1, 0)
    is_teller = jnp.logical_and(comp >= 2, x == 1)
    is_late_sky = jnp.logical_and(is_sky, half == 1)
    is_early = jnp.logical_and(half == 0, tile < tiles // 2)
    is_hub = jnp.logical_and(first, half == 0)
    x_peers = [half * 4 + lax.rem(x + k, 4) for k in range(1, 4)]
    other = lax.rem(lev + 4, 8)

    def group(g, k):
        return {"tile": (tiles - 1) * (g % 2), "lev": (g // 2) * 4 + k}

    pairs = (
        (t_hbm, t40), (u_hbm, u40), (d_hbm, d40), (q_hbm, qin), (m_hbm, m_v),
        (w_hbm, w_v), (i_hbm, i_v), (i_hbm, i_s), (sea_hbm, sea_v),
    )
    loads = [pltpu.make_async_copy(a, b, in_sem.at[k]) for k, (a, b) in enumerate(pairs)]
    for c in loads:
        c.start()

    bar = pltpu.get_barrier_semaphore()

    def hello(**where):
        pl.semaphore_signal(bar, inc=1, device_id=where, device_id_type=MESH)

    @pl.when(tile > 0)
    def _():
        hello(tile=tile - 1)

    @pl.when(tile < tiles - 1)
    def _():
        hello(tile=tile + 1)

    for p in x_peers:
        hello(lev=p)

    @pl.when(jnp.logical_and(half == 0, tile > 0))
    def _():
        hello(lev=lev + 4)

    @pl.when(jnp.logical_and(half == 1, first))
    def _():
        hello(tile=tiles - 1, lev=x)

    @pl.when(is_sky)
    def _():
        hello(comp=comp + 2, lev=half * 4 + 1)

    @pl.when(is_hub)
    def _():
        for g in (1, 3):
            for k in range(4):
                hello(**group(g, k))

    @pl.when(is_target)
    def _():
        def body(k, _):
            for j in (1, 5):

                @pl.when(jnp.logical_or(k > 0, j > 1))
                def _():
                    hello(tile=lax.rem(tile + k, tiles), lev=j)

            return 0

        lax.fori_loop(0, tiles, body, 0)

    lane = iota((16, 128), 1)

    blank = jnp.zeros((16, 640), F32)
    for k in range(3):
        ext[k] = blank
    for c in loads[:3]:
        c.wait()
    for k, ref in enumerate((t40, u40, d40)):
        for c in range(4):
            ext[k, 0:10, c * 128 : (c + 1) * 128] = ref[pl.ds(c, 10, stride=4), :]
    ends = [ext[k, :, 384:512] for k in range(3)]
    starts = [ext[k, :, 0:128] for k in range(3)]
    sendA[0] = jnp.where(
        lane >= 124, ends[0], jnp.where(lane >= 120, pltpu.roll(ends[1], 124, 1), pltpu.roll(ends[2], 120, 1))
    )
    sendA[1] = jnp.where(
        lane < 4, starts[0], jnp.where(lane < 8, pltpu.roll(starts[1], 4, 1), pltpu.roll(starts[2], 8, 1))
    )
    loads[3].wait()
    lane40 = iota((40, 128), 1)
    low40 = lane40 < 64
    zero40 = jnp.zeros((40, 128), F32)

    def pack(r, carry):
        to_right, to_left = carry
        mine = jnp.logical_and(lane40 >= 2 * r, lane40 < 2 * r + 2)
        to_right = jnp.where(mine, pltpu.roll(qin[r, :, 384:512], 2 * r + 2, 1), to_right)
        to_left = jnp.where(mine, pltpu.roll(qin[r, :, 0:128], 2 * r, 1), to_left)
        return to_right, to_left

    to_right, to_left = lax.fori_loop(0, 10, pack, (zero40, zero40))
    sendB[0] = to_right
    sendB[1] = to_left

    @pl.when(first)
    def _():
        haloA[0] = jnp.zeros((16, 128), F32)
        haloB[0] = zero40

    @pl.when(last)
    def _():
        haloA[1] = jnp.zeros((16, 128), F32)
        haloB[1] = zero40

    greeted = (
        jnp.where(tile > 0, 1, 0) + jnp.where(tile < tiles - 1, 1, 0) + 3 + jnp.where(first, 0, half)
        + jnp.where(is_teller, tiles + 4 - jnp.where(half == 0, 1, 0), 0) + jnp.where(last, 5 - half, 0)
    )
    pl.semaphore_wait(bar, greeted)

    @pl.when(tile < tiles - 1)
    def _():
        send(sendA.at[0], haloA.at[0], sA.at[0], rA.at[0], tile=tile + 1)
        send(sendB.at[0], haloB.at[0], sB.at[0], rB.at[0], tile=tile + 1)

    @pl.when(tile > 0)
    def _():
        send(sendA.at[1], haloA.at[1], sA.at[1], rA.at[1], tile=tile - 1)
        send(sendB.at[1], haloB.at[1], sB.at[1], rB.at[1], tile=tile - 1)

    @pl.when(jnp.logical_and(half == 0, last))
    def _():
        where = {"tile": 0, "lev": 4 + x}
        pl.semaphore_signal(hub_up, inc=1, device_id=where, device_id_type=MESH)

    @pl.when(jnp.logical_and(half == 1, tile > 0))
    def _():
        pl.semaphore_signal(ready, inc=1, device_id={"lev": lev - 4}, device_id_type=MESH)

    @pl.when(is_teller)
    def _():
        for k in range(4):
            where = {"comp": comp - 2, "lev": half * 4 + k}
            pl.semaphore_signal(go, inc=1, device_id=where, device_id_type=MESH)

    loads[4].wait()
    i, j = iota((48, 80), 0), iota((48, 80), 1)
    wanted = jnp.where(i < 16, lev * 10 + i, jnp.where(i < 32, other * 10 + i - 16, i - 32))
    used = jnp.where(i < 16, i, jnp.where(i < 32, i - 16, i - 23)) < 10
    pick_rows = jnp.where(jnp.logical_and(used, wanted == j), 1.0, 0.0).astype(F32)

    def pick_cols(count, start):
        i, j = iota((80, count), 0), iota((80, count), 1)
        r = lax.rem(j, 16)
        return jnp.where(jnp.logical_and(r < 10, i == start + (j // 16) * 10 + r), 1.0, 0.0).astype(F32)

    @pl.when(is_wrap)
    def _():
        edge = jnp.where(last, sendA[0], sendA[1])
        q3 = pltpu.roll(jnp.where(last, qin[0, 0:8, 384:512], qin[0, 0:8, 0:128]), 2, 0)
        ring[order, x, 0:8] = edge[0:8]
        ring[order, x, 8:16] = jnp.where(iota((8, 128), 0) < 2, edge[8:16], q3)
        mine = ring.at[order, x]

        @pl.when(order == 0)
        def _():
            for p in x_peers:
                send(mine, mine, sE.at[0], rE.at[0], lev=p)

        @pl.when(last)
        def _():
            for k in range(4):
                send(mine, mine, sE.at[0], rE.at[order], **group(0, k))

        @pl.when(order == 1)
        def _():
            send(sendB.at[0], wrapB, sW, rW, tile=0)

        @pl.when(order == 3)
        def _():
            send(sendB.at[0], relayB.at[1], sW, rV.at[1], tile=0, lev=x)

    here = jnp.logical_and(iota((16, 80), 0) < 10, iota((16, 80), 1) == lev * 10 + iota((16, 80), 0))
    top_row = jnp.broadcast_to(m_v[0:1, :], (16, 80))
    scale = jnp.sum(jnp.where(here, top_row, 0.0), axis=1, keepdims=True)
    picked = dot(pick_rows, m_v[...])
    matrix = dot(picked, pick_cols(64, half * 40))

    @pl.when(is_wrap)
    def _():
        mixed_rows[...] = dot(picked[0:32], pick_cols(128, 0))


    @pl.when(tile > 0)
    def _():
        drain(haloA.at[0], rA.at[0])

    @pl.when(tile < tiles - 1)
    def _():
        drain(haloA.at[1], rA.at[1])

    for k, block in enumerate(joined(haloA[1], haloA[0])):
        ext[k, :, 512:640] = block
    sky = jnp.where(is_sky, 1.0, 0.0).astype(F32)
    up, un = courant(ext[1])
    coef[0] = up
    coef[1] = un
    coef[2] = up * sky
    coef[3] = un * sky
    heat = heat_step(ext[0], up, un, ext[2])
    heat = heat_step(heat, up * sky, un * sky, ext[2] * sky)[:, 0:512]

    @pl.when(is_late_sky)
    def _():
        part = jnp.sum(heat * scale, axis=0, keepdims=True)
        for c in range(4):
            parts[c] = part[:, c * 128 : (c + 1) * 128]
        landed[x] = parts[x]
        for k in range(3):
            send(parts.at[lax.rem(x + k + 1, 4)], landed.at[x], sT.at[k], rT.at[k], lev=x_peers[k])

    def level(r):
        edge = jnp.where(
            low40,
            pltpu.roll(haloB[1], lax.rem(128 - 2 * r, 128), 1),
            pltpu.roll(haloB[0], 126 - 2 * r, 1),
        )
        q = jnp.concatenate([qin[r], edge], axis=1)
        up, un, up2, un2 = (jnp.broadcast_to(coef[k, pl.ds(r, 1), :], (40, 640)) for k in range(4))
        q = tracer_step(tracer_step(q, up, un), up2, un2)
        qout[r] = q[:, 0:512]

    def tracers_inside():
        def more(r, _):
            level(r)
            return 0

        lax.fori_loop(1, 10, more, 0)

    row8 = iota((8, 512), 0)
    gath[x, 0:8, :] = heat[0:8]
    gath[x, 8:16, :] = jnp.where(row8 < 2, heat[8:16], 0.0)

    def share():
        for k in range(3):
            send(gath.at[x], gath.at[x], sX.at[k], rX.at[k], lev=x_peers[k])

    @pl.when(half == 1)
    def _():
        share()

    @pl.when(jnp.logical_and(half == 1, first))
    def _():
        pl.semaphore_wait(hub_up, 1)
        pl.semaphore_signal(ready, inc=1, device_id={"lev": lev - 4}, device_id_type=MESH)
        mine = ring.at[2, x]
        for k in range(4):
            send(mine, mine, sE.at[0], rE.at[2], **group(0, k))
        send(sendB.at[1], relayB.at[0], sW, rV.at[0], tile=0, lev=x)

    @pl.when(tile > 0)
    def _():
        drain(haloB.at[0], rB.at[0])

    @pl.when(tile < tiles - 1)
    def _():
        drain(haloB.at[1], rB.at[1])

    level(0)

    @pl.when(half == 0)
    def _():
        rows_q = pltpu.roll(qout[0, 0:8, :], 2, 0)
        gath[x, 8:16, :] = jnp.where(row8 < 2, heat[8:16], jnp.where(row8 < 5, rows_q, 0.0))
        share()

    def late_rows(start, stop):
        def body(k, _):
            send(piece, pieces.at[x, tile], sP, rP, comp=comp + 2, tile=k, lev=0)
            return 0

        lax.fori_loop(start, stop, body, 0)

    @pl.when(is_late_sky)
    def _():
        for k in range(3):
            drain(landed.at[k], rT.at[k])
        piece[...] = landed[0] + landed[1] + landed[2] + landed[3]
        pl.semaphore_wait(go, 1)
        late_rows(0, 8)

    for k in range(3):
        drain(gath.at[k], rX.at[k])
    product = dot(matrix, jnp.concatenate([gath[k] for k in range(4)], axis=0))
    top = product[32:33, :]

    @pl.when(is_early)
    def _():
        tracers_inside()

    @pl.when(jnp.logical_and(is_sky, half == 0))
    def _():
        pl.semaphore_wait(go, 1)
        line = jnp.where(
            x == 0, gath[0, 10:11, :], jnp.where(x == 1, gath[0, 11:12, :], jnp.where(x == 2, gath[0, 12:13, :], top))
        )
        for c in range(4):
            srow[c : c + 1, :] = line[:, c * 128 : (c + 1) * 128]

        def body(k, _):
            send(srow, rows.at[x, tile], sR, rR, comp=comp + 2, tile=lax.rem(tile + k, tiles), lev=0)
            return 0

        lax.fori_loop(0, tiles, body, 0)

    own[...] = product[0:16]
    for c in range(4):
        flip_s[pl.ds(c, 10, stride=4), :] = product[16:26, c * 128 : (c + 1) * 128]

    @pl.when(half == 1)
    def _():
        send(flip_s, flip_r, sF, rF, lev=other)

    @pl.when(is_late_sky)
    def _():
        late_rows(8, tiles)

    def edge_heat(from_right, from_left, again):
        t, u, d = joined(from_right, from_left)
        up, un = courant(u)
        return heat_step(heat_step(t, up, un, d), up * again, un * again, d * again)

    @pl.when(is_hub)
    def _():
        drain(ring.at[0, pl.ds(0, 3)], rE.at[0])
        for g in range(1, 4):
            drain(ring.at[g], rE.at[g])
        stepped = [edge_heat(ring[2 * (k // 4), k % 4], ring[2 * (k // 4) + 1, k % 4], sky) for k in range(8)]
        mixed = dot(mixed_rows[...], jnp.concatenate(stepped, axis=0))
        mixed_v[...] = mixed[0:16]

        @pl.when(jnp.logical_and(is_sky, lev == 0))
        def _():
            q, u, _ = joined(ring[0, 0], ring[1, 0])
            up, un = courant(jnp.broadcast_to(u[0:1], (8, 128)))
            edge_s[...] = tracer_step(tracer_step(q[8:16], up, un), up, un)
            edge_s[0:1, :] = mixed_v[0:1, :]

            def body(k, _):
                send(edge_s, edge_rows, sG, rG, comp=comp + 2, tile=k, lev=0)
                return 0

            lax.fori_loop(0, tiles, body, 0)

        answer[0, 0] = mixed[0:16]
        answer[1, 0] = mixed[16:32]
        answer[2, 0] = mixed[16:32]
        answer[0, 1] = ring[0, x]
        answer[1, 1] = ring[3, x]
        answer[2, 1] = ring[2, x]
        for g in range(1, 4):
            send(answer.at[g - 1], reply, sE.at[g], rE.at[0], **group(g, x))
        for k in range(2):
            drain(relayB.at[k], rV.at[k])
        for g, edge in ((1, sendB.at[1]), (2, relayB.at[1]), (3, relayB.at[0])):
            send(edge, wrapB, sV.at[g - 1], rW, **group(g, x))

    @pl.when(jnp.logical_not(is_early))
    def _():
        tracers_inside()

    @pl.when(half == 0)
    def _():
        pl.semaphore_wait(ready, 1)
        send(flip_s, flip_r, sF, rF, lev=other)

    for c in loads[5:]:
        c.wait()

    @pl.when(jnp.logical_and(is_wrap, order > 0))
    def _():
        drain(reply, rE.at[0])
        mixed_v[...] = reply[0]
        ring[half * 2 + jnp.where(last, 0, 1), x] = reply[1]

    @pl.when(is_wrap)
    def _():
        drain(wrapB, rW)
        up, un = courant(joined(ring[half * 2, x], ring[half * 2 + 1, x])[1])
        ring_coef[0] = up
        ring_coef[1] = un
        ring_coef[2] = up * sky
        ring_coef[3] = un * sky
        for flag, c, turn in ((first, 0, 126), (last, 3, 128)):

            @pl.when(flag)
            def _():
                def fix(r, _):
                    at = slice(c * 128, (c + 1) * 128)
                    far = pltpu.roll(wrapB[...], lax.rem(turn - 2 * r, 128), 1)
                    q = jnp.where(low40, qin[r, :, at], far) if c == 0 else jnp.where(low40, far, qin[r, :, at])
                    up, un, up2, un2 = (
                        jnp.broadcast_to(ring_coef[k, pl.ds(r, 1), :], (40, 128)) for k in range(4)
                    )
                    q = tracer_step(tracer_step(q, up, un), up2, un2)
                    new = lane40 < 2 if c == 0 else lane40 >= 126
                    qout[r, :, at] = jnp.where(new, q, qout[r, :, at])
                    return 0

                lax.fori_loop(0, 10, fix, 0)

    block = lax.shift_right_logical(i_s[0, 256], 9)
    before, after = lax.rem(block + tiles - 1, tiles), lax.rem(block + 1, tiles)
    lane1 = iota((1, 128), 1)

    def window(f):
        b, m, a = rows[f, before], rows[f, block], rows[f, after]
        w = [b[3:4]] + [m[c : c + 1] for c in range(4)] + [a[0:1]]
        if f == 3:
            extra = [pieces[3, before]] + [pieces[c, block] for c in range(4)] + [pieces[0, after]]
            w = [a + b for a, b in zip(w, extra)]
        edge = edge_rows[0:1, :] if f == 3 else edge_rows[2 + f : 3 + f, :]
        w[0] = jnp.where(lane1 >= jnp.where(before == tiles - 1, 126, 128), edge, w[0])
        w[1] = jnp.where(lane1 < jnp.where(block == 0, 2, 0), edge, w[1])
        w[4] = jnp.where(lane1 >= jnp.where(block == tiles - 1, 126, 128), edge, w[4])
        w[5] = jnp.where(lane1 < jnp.where(after == 0, 2, 0), edge, w[5])
        return w

    def remap(pair):
        windows = [window(f) for f in pair]
        for c in range(4):
            at = slice(c * 128, (c + 1) * 128)
            place = jnp.bitwise_and(i_v[:, at] - block * 512 + 128, tiles * 512 - 1)
            place = jnp.concatenate([place, place], axis=0)
            which, within = lax.shift_right_logical(place, 7), jnp.bitwise_and(place, 127)
            weight = w_v[:, at]
            sea = sea_v[c : c + 1, :] == 1
            got = jnp.zeros((8, 128), F32)
            for m in range(c, c + 3):
                source = jnp.concatenate([jnp.broadcast_to(w[m], (4, 128)) for w in windows], axis=0)
                taken = jnp.take_along_axis(source, within, axis=1, mode="promise_in_bounds")
                got = jnp.where(which == m, taken, got)
            for k, f in enumerate(pair):
                remapped = jnp.sum(got[4 * k : 4 * k + 4] * weight, axis=0, keepdims=True)
                if f < 3:
                    s = qout[0, f : f + 1, at]
                    qout[0, f : f + 1, at] = jnp.where(sea, s + 0.5 * (remapped - s), s)
                else:
                    s = tout[c : c + 1, :]
                    tout[c : c + 1, :] = jnp.where(sea, s + 0.5 * (remapped - s), s)

    @pl.when(is_target)
    def _():
        drain(edge_rows, rG)
        drain(rows, rR)
        remap((0, 1))

    drain(flip_r, rF)
    for c in range(4):
        tout[pl.ds(c, 10, stride=4), :] = own[0:10, c * 128 : (c + 1) * 128] + flip_r[pl.ds(c, 10, stride=4), :]

    @pl.when(is_wrap)
    def _():
        mixed = mixed_v[0:10, :]
        for flag, c, new in ((first, 0, lane < 2), (last, 3, lane >= 126)):

            @pl.when(flag)
            def _():
                tout[pl.ds(c, 10, stride=4), :] = jnp.where(new[0:10], mixed, tout[pl.ds(c, 10, stride=4), :])

    @pl.when(is_target)
    def _():
        drain(pieces, rP)
        remap((2, 3))

    @pl.when(tile < tiles - 1)
    def _():
        drain(sendA.at[0], sA.at[0])
        drain(sendB.at[0], sB.at[0])

    @pl.when(tile > 0)
    def _():
        drain(sendA.at[1], sA.at[1])
        drain(sendB.at[1], sB.at[1])

    for k in range(3):
        drain(gath.at[k], sX.at[k])
    drain(flip_s, sF)

    @pl.when(jnp.logical_and(is_sky, half == 0))
    def _():
        drain(rows.at[0], sR)

    @pl.when(jnp.logical_and(is_sky, half == 1))
    def _():
        drain(pieces.at[0], sP)
        for k in range(3):
            drain(parts.at[k], sT.at[k])

    @pl.when(is_wrap)
    def _():
        @pl.when(order > 0)
        def _():
            drain(ring.at[0], sE.at[0])
            drain(wrapB, sW)

        @pl.when(order == 0)
        def _():
            drain(ring.at[0, pl.ds(0, 3)], sE.at[0])
            for g in range(1, 4):
                drain(reply, sE.at[g])
                drain(wrapB, sV.at[g - 1])

        @pl.when(jnp.logical_and(is_sky, jnp.logical_and(first, lev == 0)))
        def _():
            drain(rows.at[0], sG)
            drain(rows.at[0], sG)


def body(t, u, q, d, m, w, i, sea):
    hbm = pl.BlockSpec(memory_space=pltpu.HBM)
    vmem = pl.BlockSpec(memory_space=pltpu.VMEM)
    dma = pltpu.SemaphoreType.DMA
    tiles = lax.axis_size("tile")
    buf = lambda *s: pltpu.VMEM(s, F32)
    tout, qout = pl.pallas_call(
        kernel,
        out_shape=(jax.ShapeDtypeStruct((40, 128), F32), jax.ShapeDtypeStruct((10, 40, 512), F32)),
        in_specs=[hbm] * 8,
        out_specs=(vmem, vmem),
        scratch_shapes=[
            buf(40, 128), buf(40, 128), buf(40, 128), buf(10, 40, 512), buf(80, 80),
            buf(4, 512), pltpu.VMEM((4, 512), jnp.int32), pltpu.SMEM((4, 512), jnp.int32), pltpu.VMEM((4, 128), jnp.int32),
            buf(3, 16, 640), buf(4, 16, 640), buf(2, 16, 128), buf(2, 40, 128), buf(2, 16, 128), buf(2, 40, 128),
            buf(4, 16, 512), buf(40, 128), buf(40, 128), buf(16, 512), buf(4, 128), buf(1, 128),
            buf(4, tiles, 4, 128), buf(4, tiles, 1, 128),
            buf(4, 4, 16, 128), buf(4, 16, 128), buf(40, 128), buf(8, 128), buf(8, 128), buf(32, 128), buf(16, 128),
            buf(2, 40, 128), buf(3, 2, 16, 128), buf(2, 16, 128), buf(4, 1, 128), buf(4, 1, 128),
            dma((9,)), dma((2,)), dma((2,)), dma((2,)), dma((2,)), dma((3,)), dma((3,)), dma, dma,
            dma, dma, dma, dma, dma((4,)), dma((4,)), dma, dma, dma, dma, dma((3,)), dma((2,)), dma((3,)), dma((3,)), pltpu.SemaphoreType.REGULAR, pltpu.SemaphoreType.REGULAR, pltpu.SemaphoreType.REGULAR,
        ],
        compiler_params=pltpu.CompilerParams(
            collective_id=0, has_side_effects=True, vmem_limit_bytes=24 * 1024 * 1024
        ),
    )(
        *(
            pltpu.with_memory_space_constraint(v, pltpu.HBM)
            for v in (
                t.reshape(40, 128), u.reshape(40, 128), d.reshape(40, 128), jnp.transpose(q[0], (1, 0, 2)),
                m[0], w.T, i.T, sea.reshape(4, 128),
            )
        )
    )
    return tout.reshape(1, 10, 512), jnp.transpose(qout, (1, 0, 2))[None]


def solution(mesh):
    in_specs = (
        P("comp", "lev", "tile"),
        P("comp", "lev", "tile"),
        P("comp", None, "lev", "tile"),
        P("comp", "lev", "tile"),
        P("comp", None, None),
        P("tile", None),
        P("tile", None),
        P("tile"),
    )
    out_specs = (P("comp", "lev", "tile"), P("comp", None, "lev", "tile"))
    return jax.shard_map(body, mesh=mesh, in_specs=in_specs, out_specs=out_specs, check_vma=False)
```

```python
import functools

import jax
import jax.numpy as jnp
from jax import lax
from jax.experimental import pallas as pl
from jax.experimental.pallas import tpu as pltpu
from jax.sharding import PartitionSpec as P

MESH = pl.DeviceIdType.MESH
F32 = jnp.float32
HIGHEST = lax.Precision.HIGHEST


def dot(a, b):
    return jnp.dot(a, b, precision=HIGHEST, preferred_element_type=F32)


def flux(q, up, un):
    n = q.shape[1]
    return up * q + un * pltpu.roll(q, n - 1, 1)


def tracer_step(q, up, un):
    f = flux(q, up, un)
    return q - (f - pltpu.roll(f, 1, 1))


def heat_step(t, up, un, d):
    n = t.shape[1]
    f = flux(t, up, un)
    return t + (
        -(f - pltpu.roll(f, 1, 1)) + d * (pltpu.roll(t, 1, 1) - 2.0 * t + pltpu.roll(t, n - 1, 1))
    )


def drain(ref, sem):
    pltpu.make_async_copy(ref, ref, sem).wait()


def send(src, dst, s, r, **where):
    pltpu.make_async_remote_copy(
        src_ref=src, dst_ref=dst, send_sem=s, recv_sem=r, device_id=where, device_id_type=MESH
    ).start()


def iota(shape, dim):
    return lax.broadcasted_iota(jnp.int32, shape, dim)


def joined(from_right, from_left):
    low = iota((16, 128), 1) < 64
    return (
        jnp.where(low, from_right, from_left),
        jnp.where(low, pltpu.roll(from_right, 124, 1), pltpu.roll(from_left, 4, 1)),
        jnp.where(low, pltpu.roll(from_right, 120, 1), pltpu.roll(from_left, 8, 1)),
    )


def courant(u):
    return jnp.maximum(u, 0.0), jnp.minimum(u, 0.0)


def kernel(
    t_hbm, u_hbm, d_hbm, q_hbm, m_hbm, w_hbm, i_hbm, sea_hbm,
    tout, qout,
    t40, u40, d40, qin, m_v, w_v, i_v, i_s, sea_v,
    ext, coef, sendA, sendB, haloA, haloB, gath, flip_s, flip_r, own, srow, piece, rows, pieces,
    ring, ring_coef, wrapB, edge_s, edge_rows, mixed_rows, mixed_v, relayB, answer, reply, parts, landed,
    in_sem, sA, rA, sB, rB, sX, rX, sF, rF, sR, rR, sP, rP, sE, rE, sW, rW, sG, rG, sV, rV, sT, rT, ready, go, hub_up,
):
    comp, tile, lev = lax.axis_index("comp"), lax.axis_index("tile"), lax.axis_index("lev")
    tiles = lax.axis_size("tile")
    half, x = lev // 4, lax.rem(lev, 4)
    is_sky = comp < 2
    is_target = jnp.logical_and(comp >= 2, lev == 0)
    first, last = tile == 0, tile == tiles - 1
    is_wrap = jnp.logical_or(first, last)
    order = half * 2 + jnp.where(last, 1, 0)
    is_teller = jnp.logical_and(comp >= 2, x == 1)
    is_late_sky = jnp.logical_and(is_sky, half == 1)
    is_early = jnp.logical_and(half == 0, tile < tiles // 2)
    is_hub = jnp.logical_and(first, half == 0)
    x_peers = [half * 4 + lax.rem(x + k, 4) for k in range(1, 4)]
    other = lax.rem(lev + 4, 8)

    def group(g, k):
        return {"tile": (tiles - 1) * (g % 2), "lev": (g // 2) * 4 + k}

    pairs = (
        (t_hbm, t40), (u_hbm, u40), (d_hbm, d40), (q_hbm, qin), (m_hbm, m_v),
        (w_hbm, w_v), (i_hbm, i_v), (i_hbm, i_s), (sea_hbm, sea_v),
    )
    loads = [pltpu.make_async_copy(a, b, in_sem.at[k]) for k, (a, b) in enumerate(pairs)]
    for c in loads:
        c.start()

    bar = pltpu.get_barrier_semaphore()

    def hello(**where):
        pl.semaphore_signal(bar, inc=1, device_id=where, device_id_type=MESH)

    @pl.when(tile > 0)
    def _():
        hello(tile=tile - 1)

    @pl.when(tile < tiles - 1)
    def _():
        hello(tile=tile + 1)

    for p in x_peers:
        hello(lev=p)

    @pl.when(jnp.logical_and(half == 0, tile > 0))
    def _():
        hello(lev=lev + 4)

    @pl.when(jnp.logical_and(half == 1, first))
    def _():
        hello(tile=tiles - 1, lev=x)

    @pl.when(is_sky)
    def _():
        hello(comp=comp + 2, lev=half * 4 + 1)

    @pl.when(is_hub)
    def _():
        for g in (1, 3):
            for k in range(4):
                hello(**group(g, k))

    @pl.when(is_target)
    def _():
        def body(k, _):
            for j in (1, 5):

                @pl.when(jnp.logical_or(k > 0, j > 1))
                def _():
                    hello(tile=lax.rem(tile + k, tiles), lev=j)

            return 0

        lax.fori_loop(0, tiles, body, 0)

    lane = iota((16, 128), 1)

    blank = jnp.zeros((16, 640), F32)
    for k in range(3):
        ext[k] = blank
    for c in loads[:3]:
        c.wait()
    for k, ref in enumerate((t40, u40, d40)):
        for c in range(4):
            ext[k, 0:10, c * 128 : (c + 1) * 128] = ref[pl.ds(c, 10, stride=4), :]
    ends = [ext[k, :, 384:512] for k in range(3)]
    starts = [ext[k, :, 0:128] for k in range(3)]
    sendA[0] = jnp.where(
        lane >= 124, ends[0], jnp.where(lane >= 120, pltpu.roll(ends[1], 124, 1), pltpu.roll(ends[2], 120, 1))
    )
    sendA[1] = jnp.where(
        lane < 4, starts[0], jnp.where(lane < 8, pltpu.roll(starts[1], 4, 1), pltpu.roll(starts[2], 8, 1))
    )
    loads[3].wait()
    lane40 = iota((40, 128), 1)
    low40 = lane40 < 64
    zero40 = jnp.zeros((40, 128), F32)

    def pack(r, carry):
        to_right, to_left = carry
        mine = jnp.logical_and(lane40 >= 2 * r, lane40 < 2 * r + 2)
        to_right = jnp.where(mine, pltpu.roll(qin[r, :, 384:512], 2 * r + 2, 1), to_right)
        to_left = jnp.where(mine, pltpu.roll(qin[r, :, 0:128], 2 * r, 1), to_left)
        return to_right, to_left

    to_right, to_left = lax.fori_loop(0, 10, pack, (zero40, zero40))
    sendB[0] = to_right
    sendB[1] = to_left

    @pl.when(first)
    def _():
        haloA[0] = jnp.zeros((16, 128), F32)
        haloB[0] = zero40

    @pl.when(last)
    def _():
        haloA[1] = jnp.zeros((16, 128), F32)
        haloB[1] = zero40

    greeted = (
        jnp.where(tile > 0, 1, 0) + jnp.where(tile < tiles - 1, 1, 0) + 3 + jnp.where(first, 0, half)
        + jnp.where(is_teller, tiles + 4 - jnp.where(half == 0, 1, 0), 0) + jnp.where(last, 5 - half, 0)
    )
    pl.semaphore_wait(bar, greeted)

    @pl.when(tile < tiles - 1)
    def _():
        send(sendA.at[0], haloA.at[0], sA.at[0], rA.at[0], tile=tile + 1)
        send(sendB.at[0], haloB.at[0], sB.at[0], rB.at[0], tile=tile + 1)

    @pl.when(tile > 0)
    def _():
        send(sendA.at[1], haloA.at[1], sA.at[1], rA.at[1], tile=tile - 1)
        send(sendB.at[1], haloB.at[1], sB.at[1], rB.at[1], tile=tile - 1)

    @pl.when(jnp.logical_and(half == 0, last))
    def _():
        where = {"tile": 0, "lev": 4 + x}
        pl.semaphore_signal(hub_up, inc=1, device_id=where, device_id_type=MESH)

    @pl.when(jnp.logical_and(half == 1, tile > 0))
    def _():
        pl.semaphore_signal(ready, inc=1, device_id={"lev": lev - 4}, device_id_type=MESH)

    @pl.when(is_teller)
    def _():
        for k in range(4):
            where = {"comp": comp - 2, "lev": half * 4 + k}
            pl.semaphore_signal(go, inc=1, device_id=where, device_id_type=MESH)

    loads[4].wait()
    i, j = iota((48, 80), 0), iota((48, 80), 1)
    wanted = jnp.where(i < 16, lev * 10 + i, jnp.where(i < 32, other * 10 + i - 16, i - 32))
    used = jnp.where(i < 16, i, jnp.where(i < 32, i - 16, i - 23)) < 10
    pick_rows = jnp.where(jnp.logical_and(used, wanted == j), 1.0, 0.0).astype(F32)

    def pick_cols(count, start):
        i, j = iota((80, count), 0), iota((80, count), 1)
        r = lax.rem(j, 16)
        return jnp.where(jnp.logical_and(r < 10, i == start + (j // 16) * 10 + r), 1.0, 0.0).astype(F32)

    @pl.when(is_wrap)
    def _():
        edge = jnp.where(last, sendA[0], sendA[1])
        q3 = pltpu.roll(jnp.where(last, qin[0, 0:8, 384:512], qin[0, 0:8, 0:128]), 2, 0)
        ring[order, x, 0:8] = edge[0:8]
        ring[order, x, 8:16] = jnp.where(iota((8, 128), 0) < 2, edge[8:16], q3)
        mine = ring.at[order, x]

        @pl.when(order == 0)
        def _():
            for p in x_peers:
                send(mine, mine, sE.at[0], rE.at[0], lev=p)

        @pl.when(last)
        def _():
            for k in range(4):
                send(mine, mine, sE.at[0], rE.at[order], **group(0, k))

        @pl.when(order == 1)
        def _():
            send(sendB.at[0], wrapB, sW, rW, tile=0)

        @pl.when(order == 3)
        def _():
            send(sendB.at[0], relayB.at[1], sW, rV.at[1], tile=0, lev=x)

    here = jnp.logical_and(iota((16, 80), 0) < 10, iota((16, 80), 1) == lev * 10 + iota((16, 80), 0))
    top_row = jnp.broadcast_to(m_v[0:1, :], (16, 80))
    scale = jnp.sum(jnp.where(here, top_row, 0.0), axis=1, keepdims=True)
    picked = dot(pick_rows, m_v[...])
    matrix = dot(picked, pick_cols(64, half * 40))

    @pl.when(is_wrap)
    def _():
        mixed_rows[...] = dot(picked[0:32], pick_cols(128, 0))


    @pl.when(tile > 0)
    def _():
        drain(haloA.at[0], rA.at[0])

    @pl.when(tile < tiles - 1)
    def _():
        drain(haloA.at[1], rA.at[1])

    for k, block in enumerate(joined(haloA[1], haloA[0])):
        ext[k, :, 512:640] = block
    sky = jnp.where(is_sky, 1.0, 0.0).astype(F32)
    up, un = courant(ext[1])
    coef[0] = up
    coef[1] = un
    coef[2] = up * sky
    coef[3] = un * sky
    heat = heat_step(ext[0], up, un, ext[2])
    heat = heat_step(heat, up * sky, un * sky, ext[2] * sky)[:, 0:512]

    @pl.when(is_late_sky)
    def _():
        part = jnp.sum(heat * scale, axis=0, keepdims=True)
        for c in range(4):
            parts[c] = part[:, c * 128 : (c + 1) * 128]
        landed[x] = parts[x]
        for k in range(3):
            send(parts.at[lax.rem(x + k + 1, 4)], landed.at[x], sT.at[k], rT.at[k], lev=x_peers[k])

    def level(r):
        edge = jnp.where(
            low40,
            pltpu.roll(haloB[1], lax.rem(128 - 2 * r, 128), 1),
            pltpu.roll(haloB[0], 126 - 2 * r, 1),
        )
        q = jnp.concatenate([qin[r], edge], axis=1)
        up, un, up2, un2 = (jnp.broadcast_to(coef[k, pl.ds(r, 1), :], (40, 640)) for k in range(4))
        q = tracer_step(tracer_step(q, up, un), up2, un2)
        qout[r] = q[:, 0:512]

    def tracers_inside():
        def more(r, _):
            level(r)
            return 0

        lax.fori_loop(1, 10, more, 0)

    row8 = iota((8, 512), 0)
    gath[x, 0:8, :] = heat[0:8]
    gath[x, 8:16, :] = jnp.where(row8 < 2, heat[8:16], 0.0)

    def share():
        for k in range(3):
            send(gath.at[x], gath.at[x], sX.at[k], rX.at[k], lev=x_peers[k])

    @pl.when(half == 1)
    def _():
        share()

    @pl.when(jnp.logical_and(half == 1, first))
    def _():
        pl.semaphore_wait(hub_up, 1)
        pl.semaphore_signal(ready, inc=1, device_id={"lev": lev - 4}, device_id_type=MESH)
        mine = ring.at[2, x]
        for k in range(4):
            send(mine, mine, sE.at[0], rE.at[2], **group(0, k))
        send(sendB.at[1], relayB.at[0], sW, rV.at[0], tile=0, lev=x)

    @pl.when(tile > 0)
    def _():
        drain(haloB.at[0], rB.at[0])

    @pl.when(tile < tiles - 1)
    def _():
        drain(haloB.at[1], rB.at[1])

    level(0)

    @pl.when(half == 0)
    def _():
        rows_q = pltpu.roll(qout[0, 0:8, :], 2, 0)
        gath[x, 8:16, :] = jnp.where(row8 < 2, heat[8:16], jnp.where(row8 < 5, rows_q, 0.0))
        share()

    def late_rows(start, stop):
        def body(k, _):
            send(piece, pieces.at[x, tile], sP, rP, comp=comp + 2, tile=k, lev=0)
            return 0

        lax.fori_loop(start, stop, body, 0)

    @pl.when(is_late_sky)
    def _():
        for k in range(3):
            drain(landed.at[k], rT.at[k])
        piece[...] = landed[0] + landed[1] + landed[2] + landed[3]
        pl.semaphore_wait(go, 1)
        late_rows(0, 8)

    for k in range(3):
        drain(gath.at[k], rX.at[k])
    product = dot(matrix, jnp.concatenate([gath[k] for k in range(4)], axis=0))
    top = product[32:33, :]

    @pl.when(is_early)
    def _():
        tracers_inside()

    @pl.when(jnp.logical_and(is_sky, half == 0))
    def _():
        pl.semaphore_wait(go, 1)
        line = jnp.where(
            x == 0, gath[0, 10:11, :], jnp.where(x == 1, gath[0, 11:12, :], jnp.where(x == 2, gath[0, 12:13, :], top))
        )
        for c in range(4):
            srow[c : c + 1, :] = line[:, c * 128 : (c + 1) * 128]

        def body(k, _):
            send(srow, rows.at[x, tile], sR, rR, comp=comp + 2, tile=lax.rem(tile + k, tiles), lev=0)
            return 0

        lax.fori_loop(0, tiles, body, 0)

    own[...] = product[0:16]
    for c in range(4):
        flip_s[pl.ds(c, 10, stride=4), :] = product[16:26, c * 128 : (c + 1) * 128]

    @pl.when(half == 1)
    def _():
        send(flip_s, flip_r, sF, rF, lev=other)

    @pl.when(is_late_sky)
    def _():
        late_rows(8, tiles)

    def edge_heat(from_right, from_left, again):
        t, u, d = joined(from_right, from_left)
        up, un = courant(u)
        return heat_step(heat_step(t, up, un, d), up * again, un * again, d * again)

    def wrapped_tracers():
        drain(wrapB, rW)
        up, un = courant(joined(ring[half * 2, x], ring[half * 2 + 1, x])[1])
        ring_coef[0] = up
        ring_coef[1] = un
        ring_coef[2] = up * sky
        ring_coef[3] = un * sky
        for flag, c, turn in ((first, 0, 126), (last, 3, 128)):

            @pl.when(flag)
            def _():
                def fix(r, _):
                    at = slice(c * 128, (c + 1) * 128)
                    far = pltpu.roll(wrapB[...], lax.rem(turn - 2 * r, 128), 1)
                    q = jnp.where(low40, qin[r, :, at], far) if c == 0 else jnp.where(low40, far, qin[r, :, at])
                    up, un, up2, un2 = (
                        jnp.broadcast_to(ring_coef[k, pl.ds(r, 1), :], (40, 128)) for k in range(4)
                    )
                    q = tracer_step(tracer_step(q, up, un), up2, un2)
                    new = lane40 < 2 if c == 0 else lane40 >= 126
                    qout[r, :, at] = jnp.where(new, q, qout[r, :, at])
                    return 0

                lax.fori_loop(0, 10, fix, 0)

    @pl.when(is_hub)
    def _():
        drain(ring.at[0, pl.ds(0, 3)], rE.at[0])
        drain(ring.at[1], rE.at[1])
        wrapped_tracers()
        for g in (2, 3):
            drain(ring.at[g], rE.at[g])
        stepped = [edge_heat(ring[2 * (k // 4), k % 4], ring[2 * (k // 4) + 1, k % 4], sky) for k in range(8)]
        mixed = dot(mixed_rows[...], jnp.concatenate(stepped, axis=0))
        mixed_v[...] = mixed[0:16]

        @pl.when(jnp.logical_and(is_sky, lev == 0))
        def _():
            q, u, _ = joined(ring[0, 0], ring[1, 0])
            up, un = courant(jnp.broadcast_to(u[0:1], (8, 128)))
            edge_s[...] = tracer_step(tracer_step(q[8:16], up, un), up, un)
            edge_s[0:1, :] = mixed_v[0:1, :]

            def body(k, _):
                send(edge_s, edge_rows, sG, rG, comp=comp + 2, tile=k, lev=0)
                return 0

            lax.fori_loop(0, tiles, body, 0)

        answer[0, 0] = mixed[0:16]
        answer[1, 0] = mixed[16:32]
        answer[2, 0] = mixed[16:32]
        answer[0, 1] = ring[0, x]
        answer[1, 1] = ring[3, x]
        answer[2, 1] = ring[2, x]
        for g in range(1, 4):
            send(answer.at[g - 1], reply, sE.at[g], rE.at[0], **group(g, x))
        for k in range(2):
            drain(relayB.at[k], rV.at[k])
        for g, edge in ((1, sendB.at[1]), (2, relayB.at[1]), (3, relayB.at[0])):
            send(edge, wrapB, sV.at[g - 1], rW, **group(g, x))

    @pl.when(jnp.logical_not(is_early))
    def _():
        tracers_inside()

    @pl.when(half == 0)
    def _():
        pl.semaphore_wait(ready, 1)
        send(flip_s, flip_r, sF, rF, lev=other)

    for c in loads[5:]:
        c.wait()

    @pl.when(jnp.logical_and(is_wrap, order > 0))
    def _():
        drain(reply, rE.at[0])
        mixed_v[...] = reply[0]
        ring[half * 2 + jnp.where(last, 0, 1), x] = reply[1]

    @pl.when(jnp.logical_and(is_wrap, order > 0))
    def _():
        wrapped_tracers()

    block = lax.shift_right_logical(i_s[0, 256], 9)
    before, after = lax.rem(block + tiles - 1, tiles), lax.rem(block + 1, tiles)
    lane1 = iota((1, 128), 1)

    def window(f):
        b, m, a = rows[f, before], rows[f, block], rows[f, after]
        w = [b[3:4]] + [m[c : c + 1] for c in range(4)] + [a[0:1]]
        if f == 3:
            extra = [pieces[3, before]] + [pieces[c, block] for c in range(4)] + [pieces[0, after]]
            w = [a + b for a, b in zip(w, extra)]
        edge = edge_rows[0:1, :] if f == 3 else edge_rows[2 + f : 3 + f, :]
        w[0] = jnp.where(lane1 >= jnp.where(before == tiles - 1, 126, 128), edge, w[0])
        w[1] = jnp.where(lane1 < jnp.where(block == 0, 2, 0), edge, w[1])
        w[4] = jnp.where(lane1 >= jnp.where(block == tiles - 1, 126, 128), edge, w[4])
        w[5] = jnp.where(lane1 < jnp.where(after == 0, 2, 0), edge, w[5])
        return w

    def remap(pair):
        windows = [window(f) for f in pair]
        for c in range(4):
            at = slice(c * 128, (c + 1) * 128)
            place = jnp.bitwise_and(i_v[:, at] - block * 512 + 128, tiles * 512 - 1)
            place = jnp.concatenate([place, place], axis=0)
            which, within = lax.shift_right_logical(place, 7), jnp.bitwise_and(place, 127)
            weight = w_v[:, at]
            sea = sea_v[c : c + 1, :] == 1
            got = jnp.zeros((8, 128), F32)
            for m in range(c, c + 3):
                source = jnp.concatenate([jnp.broadcast_to(w[m], (4, 128)) for w in windows], axis=0)
                taken = jnp.take_along_axis(source, within, axis=1, mode="promise_in_bounds")
                got = jnp.where(which == m, taken, got)
            for k, f in enumerate(pair):
                remapped = jnp.sum(got[4 * k : 4 * k + 4] * weight, axis=0, keepdims=True)
                if f < 3:
                    s = qout[0, f : f + 1, at]
                    qout[0, f : f + 1, at] = jnp.where(sea, s + 0.5 * (remapped - s), s)
                else:
                    s = tout[c : c + 1, :]
                    tout[c : c + 1, :] = jnp.where(sea, s + 0.5 * (remapped - s), s)

    @pl.when(is_target)
    def _():
        drain(edge_rows, rG)
        drain(rows, rR)
        remap((0, 1))

    drain(flip_r, rF)
    for c in range(4):
        tout[pl.ds(c, 10, stride=4), :] = own[0:10, c * 128 : (c + 1) * 128] + flip_r[pl.ds(c, 10, stride=4), :]

    @pl.when(is_wrap)
    def _():
        mixed = mixed_v[0:10, :]
        for flag, c, new in ((first, 0, lane < 2), (last, 3, lane >= 126)):

            @pl.when(flag)
            def _():
                tout[pl.ds(c, 10, stride=4), :] = jnp.where(new[0:10], mixed, tout[pl.ds(c, 10, stride=4), :])

    @pl.when(is_target)
    def _():
        drain(pieces, rP)
        remap((2, 3))

    @pl.when(tile < tiles - 1)
    def _():
        drain(sendA.at[0], sA.at[0])
        drain(sendB.at[0], sB.at[0])

    @pl.when(tile > 0)
    def _():
        drain(sendA.at[1], sA.at[1])
        drain(sendB.at[1], sB.at[1])

    for k in range(3):
        drain(gath.at[k], sX.at[k])
    drain(flip_s, sF)

    @pl.when(jnp.logical_and(is_sky, half == 0))
    def _():
        drain(rows.at[0], sR)

    @pl.when(jnp.logical_and(is_sky, half == 1))
    def _():
        drain(pieces.at[0], sP)
        for k in range(3):
            drain(parts.at[k], sT.at[k])

    @pl.when(is_wrap)
    def _():
        @pl.when(order > 0)
        def _():
            drain(ring.at[0], sE.at[0])
            drain(wrapB, sW)

        @pl.when(order == 0)
        def _():
            drain(ring.at[0, pl.ds(0, 3)], sE.at[0])
            for g in range(1, 4):
                drain(reply, sE.at[g])
                drain(wrapB, sV.at[g - 1])

        @pl.when(jnp.logical_and(is_sky, jnp.logical_and(first, lev == 0)))
        def _():
            drain(rows.at[0], sG)
            drain(rows.at[0], sG)


def body(t, u, q, d, m, w, i, sea):
    hbm = pl.BlockSpec(memory_space=pltpu.HBM)
    vmem = pl.BlockSpec(memory_space=pltpu.VMEM)
    dma = pltpu.SemaphoreType.DMA
    tiles = lax.axis_size("tile")
    buf = lambda *s: pltpu.VMEM(s, F32)
    tout, qout = pl.pallas_call(
        kernel,
        out_shape=(jax.ShapeDtypeStruct((40, 128), F32), jax.ShapeDtypeStruct((10, 40, 512), F32)),
        in_specs=[hbm] * 8,
        out_specs=(vmem, vmem),
        scratch_shapes=[
            buf(40, 128), buf(40, 128), buf(40, 128), buf(10, 40, 512), buf(80, 80),
            buf(4, 512), pltpu.VMEM((4, 512), jnp.int32), pltpu.SMEM((4, 512), jnp.int32), pltpu.VMEM((4, 128), jnp.int32),
            buf(3, 16, 640), buf(4, 16, 640), buf(2, 16, 128), buf(2, 40, 128), buf(2, 16, 128), buf(2, 40, 128),
            buf(4, 16, 512), buf(40, 128), buf(40, 128), buf(16, 512), buf(4, 128), buf(1, 128),
            buf(4, tiles, 4, 128), buf(4, tiles, 1, 128),
            buf(4, 4, 16, 128), buf(4, 16, 128), buf(40, 128), buf(8, 128), buf(8, 128), buf(32, 128), buf(16, 128),
            buf(2, 40, 128), buf(3, 2, 16, 128), buf(2, 16, 128), buf(4, 1, 128), buf(4, 1, 128),
            dma((9,)), dma((2,)), dma((2,)), dma((2,)), dma((2,)), dma((3,)), dma((3,)), dma, dma,
            dma, dma, dma, dma, dma((4,)), dma((4,)), dma, dma, dma, dma, dma((3,)), dma((2,)), dma((3,)), dma((3,)), pltpu.SemaphoreType.REGULAR, pltpu.SemaphoreType.REGULAR, pltpu.SemaphoreType.REGULAR,
        ],
        compiler_params=pltpu.CompilerParams(
            collective_id=0, has_side_effects=True, vmem_limit_bytes=24 * 1024 * 1024
        ),
    )(
        *(
            pltpu.with_memory_space_constraint(v, pltpu.HBM)
            for v in (
                t.reshape(40, 128), u.reshape(40, 128), d.reshape(40, 128), jnp.transpose(q[0], (1, 0, 2)),
                m[0], w.T, i.T, sea.reshape(4, 128),
            )
        )
    )
    return tout.reshape(1, 10, 512), jnp.transpose(qout, (1, 0, 2))[None]


def solution(mesh):
    in_specs = (
        P("comp", "lev", "tile"),
        P("comp", "lev", "tile"),
        P("comp", None, "lev", "tile"),
        P("comp", "lev", "tile"),
        P("comp", None, None),
        P("tile", None),
        P("tile", None),
        P("tile"),
    )
    out_specs = (P("comp", "lev", "tile"), P("comp", None, "lev", "tile"))
    return jax.shard_map(body, mesh=mesh, in_specs=in_specs, out_specs=out_specs, check_vma=False)
```
